128 devices in a mesh: grp: 2 (over core), seq: 16 (over z, x), head: 4 (over y).
Axes of the slice: x: 4, y: 4, z: 4, core: 2. Of those that a mesh axis runs over, the one named last changes fastest.
Arguments:
- enc_in: bfloat16 [2, 4096, 1024], P('grp', 'seq'), may hold values from -6 to 6
- enc_gain: float32 [1024], replicated, may hold values from 0.1 to 1.9
- w_in: bfloat16 [1024, 4096], P(None, 'head'), may hold values from -0.1875 to 0.1875
- w_out: bfloat16 [4096, 1024], P('head'), may hold values from -0.09375 to 0.09375
- w_key: bfloat16 [1024, 2048], P(None, 'head'), may hold values from -0.1875 to 0.1875
- w_value: bfloat16 [1024, 2048], P(None, 'head'), may hold values from -0.1875 to 0.1875
- dec_in: bfloat16 [2, 4096, 4096], P('grp', 'seq'), may hold values from -16 to 16
- w_query: bfloat16 [4096, 2048], P(None, 'head'), may hold values from -0.09375 to 0.09375
- w_attn_out: bfloat16 [2048, 4096], P('head'), may hold values from -0.125 to 0.125
- cotangent: bfloat16 [2, 4096, 4096], P('grp', 'seq'), may hold values from -0.75 to 0.75
- group_doc: int32 [2, 16], P('grp'), may hold values from 0 to 7, never falling along the last dimension, each value on 1 to 5 neighbouring positions
- doc_lengths: int32 [2, 8], P('grp'), may hold values from 1 to 2048, 4096 in all within a row
Outputs:
- out: bfloat16 [2, 4096, 4096], P('grp', 'seq', 'head')
- grad_w_query: float32 [4096, 2048], P(('grp', 'seq'), 'head')
- grad_w_key: float32 [1024, 2048], P(('grp', 'seq'), 'head')
- grad_w_value: float32 [1024, 2048], P(('grp', 'seq'), 'head')
- grad_w_attn_out: float32 [2048, 4096], P('head', ('grp', 'seq'))
- grad_w_in: float32 [1024, 4096], P(('grp', 'seq'), 'head')
- grad_w_out: float32 [4096, 1024], P('head', ('grp', 'seq'))
The draws below stay inside these ranges and needn't reach their ends.
Inputs may be any that keep to these rules, and one draw needn't show every extreme that they name: `group_doc`: never falls along a sequence; each of the 8 documents owns at least one group. `doc_lengths`: the lengths of a sequence sum to 4096; the largest is exactly 2048.
All inputs are finite; a program needn't handle non-finite values.
Results may differ from the reference program's by a relative error of at most 0.029.
Values may be sent and summed in bfloat16 or wider, within the bound.
A program may use at most 128 MiB of HBM per device.

```python
import math
import jax
import jax.numpy as jnp
import numpy as np
from jax import lax

E = 1024
EF = 4096
D = 4096
HEAD_DIM = 128
GROUP = 256
QDEV = 256
SEQS = 2
GROUPS = 16
CTX = 4096
QTOK = 4096
NDOC = 8
HH = 2048
N_SEQ = 16


def draw_dec_in(key, part):
    base = jnp.clip(jax.random.normal(key, (SEQS, QTOK, D), jnp.float32), -4.0, 4.0)
    return base.astype(jnp.bfloat16)


def level_of(own_key, shape, split, smallest, largest):
    factor_of = 1.0
    for dim, parts in split:
        steps = jax.random.uniform(jax.random.fold_in(jax.random.fold_in(own_key, 6), dim), (parts,), jnp.float32, smallest / len(split), largest / len(split))
        factor_of = factor_of * jnp.repeat(jnp.exp(steps), shape[dim] // parts).reshape((-1,) + (1,) * (len(shape) - 1 - dim))
    return factor_of


def split_up(amount, total, limit, skew):
    weights = [(1 << 20) // math.isqrt(rank ** skew) + 1 for rank in range(2, amount + 1)]
    surplus, counts = total - limit - (amount - 1), [1] * (amount - 1)
    while surplus > 0:
        movable = [i for i in range(amount - 1) if counts[i] < limit]
        pool, budget = sum([weights[i] for i in movable]), surplus
        for i in movable:
            addition = min(limit - counts[i], max(1, budget * weights[i] // pool), surplus)
            counts[i] = counts[i] + addition
            surplus = surplus - addition
    return np.array([limit] + counts)


def uneven(own_key, amount, total, bound, skew):
    if amount == 2:
        one = jax.random.randint(own_key, (), max(1, total - bound), min(bound, total - 1) + 1)
        return jnp.stack([one, total - one])
    lengths = jnp.asarray(split_up(amount, total, bound, skew), jnp.int32)
    couples = (amount - 1) // 2
    giver, receiver = lengths[1:1 + 2 * couples:2], lengths[2:2 + 2 * couples:2]
    room = jnp.minimum(giver - 1, bound - receiver)
    moved = jax.random.randint(jax.random.fold_in(own_key, 1), (couples,), 0, 1 << 20) % (room + 1)
    lengths = lengths.at[1:1 + 2 * couples:2].set(giver - moved).at[2:2 + 2 * couples:2].set(receiver + moved)
    return lengths[jax.random.permutation(jax.random.fold_in(own_key, 2), amount)]


def centred(rng, extent, deviation, reach, shards=(), kind=jnp.bfloat16):
    result = jax.random.normal(rng, extent, jnp.float32) * deviation
    if len(shards) > 0:
        result = level_of(rng, extent, shards, -0.22, 0.18) * result
    return jnp.clip(result, min=-reach, max=reach).astype(kind)


def setup_inputs(seed: int = 0) -> dict:
    arg_keys = jax.random.split(jax.random.key(seed), 13)
    return {
        "enc_in": centred(arg_keys[0], (SEQS, CTX, E), 1.0, 6.0, ((0, 2), (1, 16))),
        "enc_gain": jnp.clip(1.0 + 0.18 * jax.random.normal(arg_keys[1], (E,), jnp.float32), 0.1, 1.9),
        "w_in": centred(arg_keys[2], (E, EF), E ** -0.5, 0.1875, ((1, 4),)),
        "w_out": centred(arg_keys[3], (EF, E), EF ** -0.5, 0.09375, ((0, 4),)),
        "w_key": centred(arg_keys[4], (E, HH), E ** -0.5, 0.1875, ((1, 4),)),
        "w_value": centred(arg_keys[5], (E, HH), E ** -0.5, 0.1875, ((1, 4),)),
        "dec_in": draw_dec_in(jax.random.fold_in(arg_keys[12], 71), 0),
        "w_query": centred(arg_keys[7], (D, HH), D ** -0.5, 0.09375, ((1, 4),)),
        "w_attn_out": centred(arg_keys[8], (HH, D), HH ** -0.5, 0.125, ((0, 4),)),
        "cotangent": centred(arg_keys[9], (SEQS, QTOK, D), 0.05, 0.75, ((0, 2), (1, 16))),
        "group_doc": jax.vmap(lambda own: jnp.searchsorted(jnp.cumsum(uneven(own, NDOC, GROUPS, GROUPS // 4 + 1, 1)), jnp.arange(GROUPS), side="right"))(jax.random.split(arg_keys[10], SEQS)).reshape((SEQS, GROUPS)).astype(jnp.int32),
        "doc_lengths": jax.vmap(lambda own: uneven(own, NDOC, QTOK, QTOK // 2, 2))(jax.random.split(arg_keys[11], SEQS)).reshape((SEQS, NDOC)).astype(jnp.int32),
    }


epsilon = 1e-06
masked_score = -1e+30

def matmul(left_side, right_side):
    return jnp.dot(left_side, right_side, preferred_element_type=jnp.float32)

def inner_rows(left_side, right_side):
    return lax.dot_general(left_side, right_side, (((0,), (0,)), ((), ())), preferred_element_type=jnp.float32)

def inner_cols(left_side, right_side):
    return lax.dot_general(left_side, right_side, (((1,), (1,)), ((), ())), preferred_element_type=jnp.float32)

def silu_slope(argument):
    sigmoid_v = jax.nn.sigmoid(argument)
    return sigmoid_v * (1.0 + argument * (1.0 - sigmoid_v))

def rounded(term_value):
    return lax.optimization_barrier(term_value.astype(jnp.bfloat16)).astype(jnp.float32)

def split_heads(matrix, head_width):
    return matrix.reshape(matrix.shape[0], -1, head_width).transpose(1, 0, 2)

def join_heads(stacked):
    return stacked.transpose(1, 0, 2).reshape(stacked.shape[1], -1)

def one_head(query_rows, key_rows, value_rows, d_mixed, allowed, score_scale):
    scores = inner_cols(query_rows, key_rows) * score_scale
    scores = jnp.where(allowed, scores, masked_score)
    row_max = lax.optimization_barrier(jnp.max(scores, axis=1, keepdims=True))
    exp_scores = jnp.exp(scores - row_max)
    probabilities = exp_scores / lax.optimization_barrier(jnp.sum(exp_scores, axis=1, keepdims=True))
    attn_weights = probabilities.astype(jnp.bfloat16)
    mixed_rows = matmul(attn_weights, value_rows)
    d_weights = inner_cols(d_mixed, value_rows)
    inner_sum = lax.optimization_barrier(jnp.sum(probabilities * d_weights, axis=1, keepdims=True))
    d_scores = (probabilities * (d_weights - inner_sum) * score_scale).astype(jnp.bfloat16)
    d_query = matmul(d_scores, key_rows)
    d_key = inner_rows(d_scores, query_rows)
    d_value = inner_rows(attn_weights, d_mixed)
    return (mixed_rows, d_query, d_key, d_value)

def attend(queries, all_keys, values, d_mixed, allowed):
    score_scale = 1.0 / math.sqrt(HEAD_DIM)

    def per_head(head_items):
        return one_head(head_items[0], head_items[1], head_items[2], head_items[3], allowed, score_scale)
    stacked = lax.map(per_head, (split_heads(queries, HEAD_DIM), split_heads(all_keys, HEAD_DIM), split_heads(values, HEAD_DIM), split_heads(d_mixed, HEAD_DIM)))
    return (join_heads(stacked[0]), join_heads(stacked[1]), join_heads(stacked[2]), join_heads(stacked[3]))

def block_terms(left_side, right_side, block_count):
    left_blocks = left_side.reshape(block_count, -1, left_side.shape[1])
    right_blocks = right_side.reshape(block_count, -1, right_side.shape[1])

    def scan_step(running, pair):
        return (running + rounded(inner_rows(pair[0], pair[1])), None)
    start = jnp.zeros((left_side.shape[1], right_side.shape[1]), jnp.float32)
    return lax.scan(scan_step, start, (left_blocks, right_blocks))[0]

def reference(enc_in, enc_gain, w_in, w_out, w_key, w_value, dec_in, w_query, w_attn_out, cotangent, group_doc, doc_lengths):
    grad_query = jnp.zeros((D, HH), jnp.float32)
    grad_key = jnp.zeros((E, HH), jnp.float32)
    grad_value = jnp.zeros((E, HH), jnp.float32)
    grad_attn = jnp.zeros((HH, D), jnp.float32)
    grad_in = jnp.zeros((E, EF), jnp.float32)
    grad_out = jnp.zeros((EF, E), jnp.float32)
    outputs = []
    for seq_index in range(SEQS):
        encoded = enc_in[seq_index].astype(jnp.float32)
        square = lax.optimization_barrier(jnp.mean(encoded * encoded, axis=1, keepdims=True))
        normed = (encoded * lax.rsqrt(square + epsilon) * enc_gain).astype(jnp.bfloat16)
        pre_act = matmul(normed, w_in)
        activated = jax.nn.silu(pre_act).astype(jnp.bfloat16)
        enc_out = (encoded + matmul(activated, w_out)).astype(jnp.bfloat16)
        all_keys = matmul(enc_out, w_key).astype(jnp.bfloat16)
        values = matmul(enc_out, w_value).astype(jnp.bfloat16)
        doc_ends = jnp.cumsum(doc_lengths[seq_index])
        positions = jnp.arange(QTOK, dtype=jnp.int32)
        query_doc = lax.optimization_barrier(jnp.sum((positions[:, None] >= doc_ends[None, :]).astype(jnp.int32), axis=1))
        key_doc = jnp.repeat(group_doc[seq_index], GROUP)
        dec_blocks = dec_in[seq_index].reshape(N_SEQ, QDEV, D)
        cot_blocks = cotangent[seq_index].reshape(N_SEQ, QDEV, D)
        doc_blocks = query_doc.reshape(N_SEQ, QDEV)

        def scan_step(running, block_items):
            d_keys, d_values, g_query, g_attn = running
            decoder, upstream, block_doc = block_items
            queries = matmul(decoder, w_query).astype(jnp.bfloat16)
            d_mixed = inner_cols(upstream, w_attn_out).astype(jnp.bfloat16)
            allowed = block_doc[:, None] == key_doc[None, :]
            mixed_f, d_query, d_key, d_value = attend(queries, all_keys, values, d_mixed, allowed)
            mixed_b = mixed_f.astype(jnp.bfloat16)
            out_block = (decoder.astype(jnp.float32) + matmul(mixed_b, w_attn_out)).astype(jnp.bfloat16)
            d_query_b = d_query.astype(jnp.bfloat16)
            running = (d_keys + rounded(d_key), d_values + rounded(d_value), g_query + rounded(inner_rows(decoder, d_query_b)), g_attn + rounded(inner_rows(mixed_b, upstream)))
            return (running, out_block)
        start = (jnp.zeros((CTX, HH), jnp.float32), jnp.zeros((CTX, HH), jnp.float32), grad_query, grad_attn)
        running, out_blocks = lax.scan(scan_step, start, (dec_blocks, cot_blocks, doc_blocks))
        d_keys, d_values, grad_query, grad_attn = running
        outputs.append(out_blocks.reshape(QTOK, D))
        key_grad = d_keys.astype(jnp.bfloat16)
        value_grad = d_values.astype(jnp.bfloat16)
        grad_key = grad_key + block_terms(enc_out, key_grad, N_SEQ)
        grad_value = grad_value + block_terms(enc_out, value_grad, N_SEQ)
        d_enc = (inner_cols(key_grad, w_key) + inner_cols(value_grad, w_value)).astype(jnp.bfloat16)
        grad_out = grad_out + block_terms(activated, d_enc, N_SEQ)
        d_pre = (inner_cols(d_enc, w_out) * silu_slope(pre_act)).astype(jnp.bfloat16)
        grad_in = grad_in + block_terms(normed, d_pre, N_SEQ)
    return (jnp.stack(outputs), grad_query, grad_key, grad_value, grad_attn, grad_in, grad_out)
```

```python
import functools
import math

import jax
import jax.numpy as jnp
from jax import lax
from jax.experimental import pallas as pl
from jax.experimental.pallas import tpu as pltpu
from jax.sharding import PartitionSpec as P

HEAD_DIM = 128
GROUP = 256
N_SEQ = 16
N_HEAD = 4
EPSILON = 1e-06
MASKED = -1e30
SCALE = 1.0 / math.sqrt(HEAD_DIM)
MESH = pl.DeviceIdType.MESH
BF = jnp.bfloat16
F32 = jnp.float32
VMEM_LIMIT = 62 * 1024 * 1024
VM = pl.BlockSpec(memory_space=pltpu.VMEM)
ANY = pl.BlockSpec(memory_space=pl.ANY)


def mm(a, b):
    return lax.dot_general(a, b, (((1,), (0,)), ((), ())), preferred_element_type=F32)


def mm_rows(a, b):
    return lax.dot_general(a, b, (((0,), (0,)), ((), ())), preferred_element_type=F32)


def mm_cols(a, b):
    return lax.dot_general(a, b, (((1,), (1,)), ((), ())), preferred_element_type=F32)


def ring_pos(lane, s):
    z, x = lax.div(s, 4), lax.rem(s, 4)
    w = lax.rem(x + z, 4)
    p = 4 * z + w if lane < 2 else 4 * x + w
    return p if lane % 2 == 0 else lax.rem(16 - p, 16)


def ring_dev(lane, p):
    if lane % 2 == 1:
        p = lax.rem(16 - p, 16)
    a = lax.div(p, 4)
    b = lax.rem(lax.rem(p, 4) + 4 - a, 4)
    return 4 * a + b if lane < 2 else 4 * b + a


class Rings:
    def __init__(self, rows, send_sem, recv_sem):
        s = lax.axis_index("seq")
        self.rows = rows
        self.pos = [ring_pos(q, s) for q in range(4)]
        self.next = [ring_dev(q, lax.rem(self.pos[q] + 1, 16)) for q in range(4)]
        self.me = s
        self.ss, self.rs = send_sem, recv_sem

    def part(self, q):
        return pl.ds(q * self.rows, self.rows)

    def dev(self, q, back):
        return ring_dev(q, lax.rem(self.pos[q] + 32 - back, 16))

    def copy(self, q, t, src, dst):
        return pltpu.make_async_remote_copy(
            src_ref=src,
            dst_ref=dst,
            send_sem=self.ss.at[q, t],
            recv_sem=self.rs.at[q, t],
            device_id={"seq": self.next[q]},
            device_id_type=MESH,
        )


class Gather(Rings):
    def __init__(self, blocks, rows, ss, rs):
        super().__init__(rows, ss, rs)
        self.blocks = blocks

    def sending(self, q, t):
        ref = self.blocks.at[self.dev(q, t), self.part(q)]
        return self.copy(q, t, ref, ref)

    def landing(self, q, t):
        ref = self.blocks.at[self.dev(q, t + 1), self.part(q)]
        return self.copy(q, t, ref, ref)

    def start(self):
        for q in range(4):
            self.sending(q, 0).start()

    def step(self, t):
        for q in range(4):
            self.landing(q, t).wait_recv()
            self.sending(q, t + 1).start()

    def finish(self):
        for q in range(4):
            self.landing(q, 14).wait_recv()

    def drain(self):
        def body(t, c):
            for q in range(4):
                self.sending(q, t).wait_send()
            return c

        lax.fori_loop(0, 15, body, 0)


class Scatter(Rings):
    def __init__(self, blocks, slots, rows, ss, rs):
        super().__init__(rows, ss, rs)
        self.blocks, self.slots = blocks, slots

    def start(self):
        for q in range(4):
            src = self.blocks.at[self.dev(q, 1), self.part(q)]
            self.copy(q, 0, src, self.slots.at[q, 0]).start()

    def sending(self, q, t):
        return self.copy(q, t + 1, self.slots.at[q, t], self.slots.at[q, t + 1])

    def landing(self, q, t):
        return self.copy(q, t, self.slots.at[q, t], self.slots.at[q, t])

    def step(self, t):
        for q in range(4):
            self.landing(q, t).wait_recv()
            own = self.blocks[self.dev(q, t + 2), self.part(q)]
            self.slots[q, t] = (self.slots[q, t].astype(F32) + own.astype(F32)).astype(BF)
            self.sending(q, t).start()

    def finish(self, q):
        self.landing(q, 14).wait_recv()
        own = self.blocks[self.me, self.part(q)]
        return self.slots[q, 14].astype(F32) + own.astype(F32)

    def drain(self):
        for q in range(4):
            src = self.blocks.at[self.dev(q, 1), self.part(q)]
            self.copy(q, 0, src, self.slots.at[q, 0]).wait_send()

        def body(t, c):
            for q in range(4):
                self.sending(q, t).wait_send()
            return c

        lax.fori_loop(0, 14, body, 0)


def greet(with_partner):
    s = lax.axis_index("seq")
    h = lax.axis_index("head")
    barrier = pltpu.get_barrier_semaphore()
    count = 0
    for q in range(4):
        right = ring_dev(q, lax.rem(ring_pos(q, s) + 1, 16))
        pl.semaphore_signal(barrier, inc=1, device_id={"seq": right}, device_id_type=MESH)
        count += 1
    for d in range(1, 4):
        pl.semaphore_signal(
            barrier, inc=1, device_id={"head": lax.rem(h + d, 4)}, device_id_type=MESH
        )
        count += 1
    if with_partner:
        pl.semaphore_signal(
            barrier, inc=1, device_id={"grp": 1 - lax.axis_index("grp")}, device_id_type=MESH
        )
        count += 1
    pl.semaphore_wait(barrier, count)


def head_copy(d, src, dst, ss, rs):
    h = lax.axis_index("head")
    return pltpu.make_async_remote_copy(
        src_ref=src,
        dst_ref=dst,
        send_sem=ss.at[d - 1],
        recv_sem=rs.at[d - 1],
        device_id={"head": lax.rem(h + d, 4)},
        device_id_type=MESH,
    )


class HeadSum:
    def __init__(self, parts, slots, total, ss, rs, ss2, rs2):
        self.parts, self.slots, self.total = parts, slots, total
        self.ss, self.rs, self.ss2, self.rs2 = ss, rs, ss2, rs2
        self.h = lax.axis_index("head")

    def quarter(self, h):
        return pl.ds(pl.multiple_of(h * 64, 64), 64)

    def first(self, d):
        src = self.parts.at[self.quarter(lax.rem(self.h + d, 4))]
        return head_copy(d, src, self.slots.at[d - 1], self.ss, self.rs)

    def second(self, d):
        ref = self.total.at[self.quarter(self.h)]
        return head_copy(d, ref, ref, self.ss2, self.rs2)

    def second_landing(self, d):
        ref = self.total.at[self.quarter(lax.rem(self.h + 4 - d, 4))]
        return head_copy(d, ref, ref, self.ss2, self.rs2)

    def send(self):
        for d in (2, 1, 3):
            self.first(d).start()

    def receive(self):
        total = self.parts[self.quarter(self.h)].astype(F32)
        for d in (1, 3, 2):
            self.first(d).wait_recv()
            total = total + self.slots[d - 1].astype(F32)
        return total

    def share(self, total):
        self.total[self.quarter(self.h)] = total.astype(BF)
        for d in (2, 1, 3):
            self.second(d).start()

    def collect(self):
        for d in (1, 3, 2):
            self.second_landing(d).wait_recv()

    def drain(self):
        for d in (1, 2, 3):
            self.first(d).wait_send()
            self.second(d).wait_send()


def encoder_kernel(
    enc_in, gain, w_in, w_out, w_key, w_value, dec, w_query, w_attn, cot,
    normed, pre_act, activated, enc_out, kv, queries, d_mixed,
    v_in, v_out, v_key, v_value, v_dec, v_query, v_attn, v_cot, load_sem,
    parts, slots, hs1, hr1, hs2, hr2, ring_s, ring_r,
):
    pairs = (
        (w_in, v_in), (w_out, v_out), (dec, v_dec), (w_query, v_query),
        (w_key, v_key), (w_value, v_value), (cot, v_cot), (w_attn, v_attn),
    )
    loads = {id(v): pltpu.make_async_copy(a, v, load_sem.at[i]) for i, (a, v) in enumerate(pairs)}
    for copy in loads.values():
        copy.start()
    greet(False)
    seq = lax.axis_index("seq")
    encoded = enc_in[...].astype(F32)
    square = jnp.mean(encoded * encoded, axis=1, keepdims=True)
    normed[...] = (encoded * lax.rsqrt(square + EPSILON) * gain[...]).astype(BF)
    loads[id(v_in)].wait()
    for n in range(4):
        cols = pl.ds(n * 256, 256)
        pre = mm(normed[...], v_in[:, cols])
        pre_act[:, cols] = pre
        activated[:, cols] = (pre / (1.0 + jnp.exp(-pre))).astype(BF)
    loads[id(v_out)].wait()
    for n in range(4):
        cols = pl.ds(n * 256, 256)
        parts[:, cols] = mm(activated[...], v_out[:, cols]).astype(BF)
    across = HeadSum(parts, slots, enc_out, hs1, hr1, hs2, hr2)
    across.send()
    loads[id(v_dec)].wait()
    loads[id(v_query)].wait()
    for n in range(2):
        cols = pl.ds(n * 256, 256)
        queries[:, cols] = mm(v_dec[...], v_query[:, cols]).astype(BF)
    own_rows = across.quarter(across.h)
    across.share(across.receive() + enc_in[own_rows].astype(F32))
    loads[id(v_cot)].wait()
    loads[id(v_attn)].wait()
    for n in range(2):
        cols = pl.ds(n * 256, 256)
        d_mixed[:, cols] = mm_cols(v_cot[...], v_attn[cols, :]).astype(BF)
    loads[id(v_key)].wait()
    loads[id(v_value)].wait()
    across.collect()
    for n in range(2):
        cols = pl.ds(n * 256, 256)
        kv[seq, :, cols] = mm(enc_out[...], v_key[:, cols]).astype(BF)
        kv[seq, :, pl.ds(512 + n * 256, 256)] = mm(enc_out[...], v_value[:, cols]).astype(BF)
    ring = Gather(kv, 64, ring_s, ring_r)
    ring.start()

    def body(t, c):
        ring.step(t)
        return c

    lax.fori_loop(0, 14, body, 0)
    ring.finish()
    ring.drain()
    across.drain()


def run_encoder(*args):
    sds = jax.ShapeDtypeStruct
    dma = pltpu.SemaphoreType.DMA
    return pl.pallas_call(
        encoder_kernel,
        out_shape=(
            sds((256, 1024), BF), sds((256, 1024), F32), sds((256, 1024), BF), sds((256, 1024), BF),
            sds((16, 256, 1024), BF), sds((256, 512), BF), sds((256, 512), BF),
        ),
        in_specs=[VM, VM] + [ANY] * 8,
        out_specs=(VM,) * 7,
        scratch_shapes=[
            pltpu.VMEM((1024, 1024), BF), pltpu.VMEM((1024, 1024), BF),
            pltpu.VMEM((1024, 512), BF), pltpu.VMEM((1024, 512), BF),
            pltpu.VMEM((256, 4096), BF), pltpu.VMEM((4096, 512), BF),
            pltpu.VMEM((512, 4096), BF), pltpu.VMEM((256, 4096), BF), dma((8,)),
            pltpu.VMEM((256, 1024), BF), pltpu.VMEM((3, 64, 1024), BF),
            dma((3,)), dma((3,)), dma((3,)), dma((3,)), dma((4, 15)), dma((4, 15)),
        ],
        compiler_params=pltpu.CompilerParams(
            collective_id=0, has_side_effects=True, vmem_limit_bytes=VMEM_LIMIT
        ),
        cost_estimate=pl.CostEstimate(flops=5 * 10**9, bytes_accessed=30 * 2**20, transcendentals=2**18),
        name="encoder_gather",
    )(*args)


def attention_kernel(
    bounds, key_doc, query_doc, queries, d_mixed, kv_hbm, mixed, d_query, d_kv, kv, scores, acc, load_sem
):
    lo, hi = bounds[0], bounds[1]

    def load(g):
        return pltpu.make_async_copy(kv_hbm.at[g], kv.at[g], load_sem.at[g])

    def begin(g, c):
        load(g).start()
        return c

    lax.fori_loop(lo, hi, begin, 0)

    def clear(g, c):
        @pl.when((g < lo) | (g >= hi))
        def _():
            d_kv[g] = jnp.zeros((GROUP, 1024), BF)

        return c

    lax.fori_loop(0, N_SEQ, clear, 0)

    def arrive(g, c):
        load(g).wait()
        return c

    lax.fori_loop(lo, hi, arrive, 0)
    docs = query_doc[...]
    for head in range(4):
        cols = pl.ds(head * 128, 128)
        vals = pl.ds(512 + head * 128, 128)

        def score(g, m):
            s = mm_cols(queries[:, cols], kv[g, :, cols]) * SCALE
            s = jnp.where(docs == key_doc[g], s, MASKED)
            scores[g] = s
            return jnp.maximum(m, jnp.max(s, axis=1, keepdims=True))

        top = lax.fori_loop(lo, hi, score, jnp.full((256, 1), MASKED, F32))
        acc[...] = jnp.zeros((256, 128), F32)

        def weigh(g, total):
            p = jnp.exp(scores[g] - top)
            scores[g] = p
            acc[...] += mm(p.astype(BF), kv[g, :, vals])
            return total + jnp.sum(p, axis=1, keepdims=True)

        total = lax.fori_loop(lo, hi, weigh, jnp.zeros((256, 1), F32))
        inverse = 1.0 / total
        rows = acc[...] * inverse
        mixed[:, cols] = rows.astype(BF)
        inner = jnp.sum(rows * d_mixed[:, cols].astype(F32), axis=1, keepdims=True)
        acc[...] = jnp.zeros((256, 128), F32)

        def back(g, c):
            p = scores[g] * inverse
            dw = mm_cols(d_mixed[:, cols], kv[g, :, vals])
            ds = (p * (dw - inner) * SCALE).astype(BF)
            acc[...] += mm(ds, kv[g, :, cols])
            d_kv[g, :, cols] = mm_rows(ds, queries[:, cols]).astype(BF)
            d_kv[g, :, vals] = mm_rows(p.astype(BF), d_mixed[:, cols]).astype(BF)
            return c

        lax.fori_loop(lo, hi, back, 0)
        d_query[:, cols] = acc[...].astype(BF)


def run_attention(bounds, key_doc, query_doc, queries, d_mixed, kv):
    sds = jax.ShapeDtypeStruct
    smem = pl.BlockSpec(memory_space=pltpu.SMEM)
    return pl.pallas_call(
        attention_kernel,
        out_shape=(sds((256, 512), BF), sds((256, 512), BF), sds((16, 256, 1024), BF)),
        in_specs=[smem, smem, VM, VM, VM, ANY],
        out_specs=(VM,) * 3,
        scratch_shapes=[
            pltpu.VMEM((16, 256, 1024), BF), pltpu.VMEM((16, 256, 256), F32),
            pltpu.VMEM((256, 128), F32), pltpu.SemaphoreType.DMA((16,)),
        ],
        compiler_params=pltpu.CompilerParams(vmem_limit_bytes=VMEM_LIMIT),
        cost_estimate=pl.CostEstimate(flops=2 * 10**9, bytes_accessed=16 * 2**20, transcendentals=2**20),
        name="attention",
    )(bounds, key_doc, query_doc, queries, d_mixed, kv)


def partner_copy(u, src, dst, ss, rs):
    return pltpu.make_async_remote_copy(
        src_ref=src,
        dst_ref=dst,
        send_sem=ss.at[u],
        recv_sem=rs.at[u],
        device_id={"grp": 1 - lax.axis_index("grp")},
        device_id_type=MESH,
    )


def decoder_kernel(
    d_kv, mixed, d_query, dec, cot, w_attn,
    out, grads, kv_grad,
    slots, ring_s, ring_r, out_own, out_send, out_recv, os, orr, stage, arrived, ps, pr,
):
    greet(True)
    ring = Scatter(d_kv, slots, 64, ring_s, ring_r)
    ring.start()
    h = lax.axis_index("head")
    grp = lax.axis_index("grp")

    def out_copy(d):
        return head_copy(d, out_send.at[d - 1], out_recv.at[d - 1], os, orr)

    def columns(owner):
        return pl.ds(pl.multiple_of(owner * 1024, 1024), 1024)

    def half(n, first):
        return pl.ds(pl.multiple_of(first + n * 256, 256), 256)

    for d in (2, 1, 3):
        first = lax.rem(h + d, 4) * 1024
        for n in range(4):
            out_send[d - 1, :, pl.ds(n * 256, 256)] = mm(mixed[...], w_attn[:, half(n, first)]).astype(BF)
        out_copy(d).start()
    ring.step(0)
    for n in range(4):
        here = half(n, h * 1024)
        out_own[:, pl.ds(n * 256, 256)] = mm(mixed[...], w_attn[:, here]) + dec[:, here].astype(F32)

    def products(u):
        t = lax.rem(u + 8 * (1 - grp), 16)
        here = pl.ds(pl.multiple_of(t * 256, 256), 256)
        return mm_rows(dec[:, here], d_query[...]), mm_rows(cot[:, here], mixed[...])

    def exchange(u):
        pair = pl.ds(2 * u, 2)
        return partner_copy(u, stage.at[pair], arrived.at[pair], ps, pr)

    def far(u, c):
        for which, term in enumerate(products(u)):
            for k in range(2):
                stage[2 * u + k, pl.ds(128 * which, 128)] = term[128 * k : 128 * (k + 1)].astype(BF)
        exchange(u).start()
        ring.step(u + 1)
        return c

    lax.fori_loop(0, 8, far, 0)

    def near(u):
        terms = products(u + 8)
        exchange(u).wait_recv()
        for which, term in enumerate(terms):
            for k in range(2):
                rows = pl.ds(128 * which, 128)
                both = term[128 * k : 128 * (k + 1)] + arrived[2 * u + k, rows].astype(F32)
                grads[2 * u + k, rows] = both.astype(BF)

    def near_step(u, c):
        near(u)
        ring.step(u + 9)
        return c

    lax.fori_loop(0, 5, near_step, 0)

    def near_only(u, c):
        near(u)
        return c

    lax.fori_loop(5, 8, near_only, 0)
    total = out_own[...]
    for d in (1, 3, 2):
        out_copy(d).wait_recv()
        total = total + out_recv[d - 1].astype(F32)
    out[...] = total.astype(BF)
    for q in range(4):
        kv_grad[pl.ds(q * 64, 64)] = ring.finish(q).astype(BF)
    ring.drain()
    for d in (1, 2, 3):
        out_copy(d).wait_send()

    def sent(u, c):
        exchange(u).wait_send()
        return c

    lax.fori_loop(0, 8, sent, 0)


def run_decoder(*args):
    sds = jax.ShapeDtypeStruct
    dma = pltpu.SemaphoreType.DMA
    return pl.pallas_call(
        decoder_kernel,
        out_shape=(sds((256, 1024), BF), sds((16, 256, 512), BF), sds((256, 1024), BF)),
        in_specs=[VM] * 6,
        out_specs=(VM,) * 3,
        scratch_shapes=[
            pltpu.VMEM((4, 15, 64, 1024), BF), dma((4, 15)), dma((4, 15)),
            pltpu.VMEM((256, 1024), F32), pltpu.VMEM((3, 256, 1024), BF), pltpu.VMEM((3, 256, 1024), BF),
            dma((3,)), dma((3,)),
            pltpu.VMEM((16, 256, 512), BF), pltpu.VMEM((16, 256, 512), BF), dma((8,)), dma((8,)),
        ],
        compiler_params=pltpu.CompilerParams(
            collective_id=1, has_side_effects=True, vmem_limit_bytes=VMEM_LIMIT
        ),
        cost_estimate=pl.CostEstimate(flops=4 * 10**9, bytes_accessed=24 * 2**20, transcendentals=0),
        name="decoder_scatter",
    )(*args)


def weights_kernel(
    grads, kv_grad, enc_out, normed, pre_act, activated, w_key, w_value, w_out,
    first, second,
    slots1, s1, r1, slots2, s2, r2, parts, slots, d_enc, hs1, hr1, hs2, hr2,
    d_pre, own, stage, arrived, ps, pr,
):
    greet(True)
    grp = lax.axis_index("grp")
    ring = Scatter(grads, slots1, 64, s1, r1)
    ring.start()
    k_grad, v_grad = kv_grad.at[:, pl.ds(0, 512)], kv_grad.at[:, pl.ds(512, 512)]
    for n in range(4):
        rows = pl.ds(n * 256, 256)
        part = mm_cols(k_grad[...], w_key[rows, :]) + mm_cols(v_grad[...], w_value[rows, :])
        parts[:, rows] = part.astype(BF)
    across = HeadSum(parts, slots, d_enc, hs1, hr1, hs2, hr2)
    across.send()
    ring.step(0)
    far, near = (1 - grp) * 512, grp * 512

    def exchange(u):
        places = (pl.ds(0, 64), pl.ds(64, 64), pl.ds(128, 64))
        return partner_copy(u, stage.at[:, places[u]], arrived.at[:, places[u]], ps, pr)

    def term(left, right, row, base):
        for n in range(2):
            cols = pl.ds(pl.multiple_of(base + n * 256, 256), 256)
            value = mm_rows(left[:, cols], right[...])
            for k in range(8):
                yield n * 8 + k, row, value[32 * k : 32 * (k + 1)]

    def put(dst, left, right, row):
        for base, target in ((far, stage), (near, own)):
            for block, place, value in term(left, right, row, base):
                target[block, pl.ds(place, 32)] = value.astype(BF)

    put(None, enc_out, k_grad, 0)
    ring.step(1)
    put(None, enc_out, v_grad, 32)
    exchange(0).start()
    ring.step(2)
    ring.step(3)
    across.share(across.receive())
    ring.step(4)
    ring.step(5)
    ring.step(6)
    across.collect()
    for n in range(4):
        cols = pl.ds(n * 256, 256)
        pre = pre_act[:, cols]
        sig = 1.0 / (1.0 + jnp.exp(-pre))
        slope = sig * (1.0 + pre * (1.0 - sig))
        d_pre[:, cols] = (mm_cols(d_enc[...], w_out[cols, :]) * slope).astype(BF)
    ring.step(7)
    for n in range(2):
        put(None, normed, d_pre.at[:, pl.ds(512 * n, 512)], 64 + 32 * n)
        ring.step(8 + n)
    exchange(1).start()
    for n in range(2):
        put(None, d_enc, activated.at[:, pl.ds(512 * n, 512)], 128 + 32 * n)
        ring.step(10 + n)
    exchange(2).start()
    ring.step(12)
    for u in range(3):
        exchange(u).wait_recv()
    ring.step(13)

    def add(b, c):
        own[b] = (own[b].astype(F32) + arrived[b].astype(F32)).astype(BF)
        return c

    lax.fori_loop(0, 16, add, 0)
    ring2 = Scatter(own, slots2, 48, s2, r2)
    ring2.start()
    for q in range(4):
        first[pl.ds(q * 64, 64)] = ring.finish(q)
    ring.drain()
    across.drain()
    for u in range(3):
        exchange(u).wait_send()

    def body(t, c):
        ring2.step(t)
        return c

    lax.fori_loop(0, 14, body, 0)
    for q in range(4):
        second[pl.ds(q * 48, 48)] = ring2.finish(q)
    ring2.drain()


def run_weights(*args):
    sds = jax.ShapeDtypeStruct
    dma = pltpu.SemaphoreType.DMA
    return pl.pallas_call(
        weights_kernel,
        out_shape=(sds((256, 512), F32), sds((192, 512), F32)),
        in_specs=[VM] * 9,
        out_specs=(VM,) * 2,
        scratch_shapes=[
            pltpu.VMEM((4, 15, 64, 512), BF), dma((4, 15)), dma((4, 15)),
            pltpu.VMEM((4, 15, 48, 512), BF), dma((4, 15)), dma((4, 15)),
            pltpu.VMEM((256, 1024), BF), pltpu.VMEM((3, 64, 1024), BF), pltpu.VMEM((256, 1024), BF),
            dma((3,)), dma((3,)), dma((3,)), dma((3,)),
            pltpu.VMEM((256, 1024), BF),
            pltpu.VMEM((16, 192, 512), BF), pltpu.VMEM((16, 192, 512), BF), pltpu.VMEM((16, 192, 512), BF),
            dma((3,)), dma((3,)),
        ],
        compiler_params=pltpu.CompilerParams(
            collective_id=2, has_side_effects=True, vmem_limit_bytes=VMEM_LIMIT
        ),
        cost_estimate=pl.CostEstimate(flops=3 * 10**9, bytes_accessed=16 * 2**20, transcendentals=2**18),
        name="weights_scatter",
    )(*args)


def shards(
    enc_in, enc_gain, w_in, w_out, w_key, w_value, dec_in, w_query, w_attn_out, cotangent, group_doc, doc_lengths,
):
    positions = lax.axis_index("seq") * 256 + jnp.arange(256, dtype=jnp.int32)
    earlier = jnp.arange(8)[:, None] <= jnp.arange(8)[None, :]
    doc_ends = jnp.sum(jnp.where(earlier, doc_lengths[0][:, None], 0), axis=0)
    query_doc = jnp.sum((positions[:, None] >= doc_ends[None, :]).astype(jnp.int32), axis=1)
    key_doc = group_doc[0]
    lo = jnp.sum((key_doc < query_doc[0]).astype(jnp.int32))
    hi = jnp.sum((key_doc <= query_doc[255]).astype(jnp.int32))
    bounds = jnp.stack([lo, hi])
    normed, pre_act, activated, enc_out, kv, queries, d_mixed = run_encoder(
        enc_in[0], enc_gain[None, :], w_in, w_out, w_key, w_value, dec_in[0], w_query, w_attn_out, cotangent[0]
    )
    mixed, d_query, d_kv = run_attention(bounds, key_doc, query_doc[:, None], queries, d_mixed, kv)
    out, grads, kv_grad = run_decoder(d_kv, mixed, d_query, dec_in[0], cotangent[0], w_attn_out)
    first, second = run_weights(
        grads, kv_grad, enc_out, normed, pre_act, activated, w_key, w_value, w_out
    )
    g_query, g_attn = first[:128], first[128:].T
    g_key, g_value = second[:32], second[32:64]
    g_in = jnp.concatenate([second[64:96], second[96:128]], axis=1)
    g_out = jnp.concatenate([second[128:160], second[160:192]], axis=1).T
    return (out[None], g_query, g_key, g_value, g_attn, g_in, g_out)


def solution(mesh):
    placed = (
        P("grp", "seq", None),
        P(),
        P(None, "head"),
        P("head", None),
        P(None, "head"),
        P(None, "head"),
        P("grp", "seq", None),
        P(None, "head"),
        P("head", None),
        P("grp", "seq", None),
        P("grp", None),
        P("grp", None),
    )
    return jax.shard_map(
        shards,
        mesh=mesh,
        in_specs=placed,
        out_specs=(
            P("grp", "seq", "head"),
            P(("grp", "seq"), "head"),
            P(("grp", "seq"), "head"),
            P(("grp", "seq"), "head"),
            P("head", ("grp", "seq")),
            P(("grp", "seq"), "head"),
            P("head", ("grp", "seq")),
        ),
        check_vma=False,
    )
```

```python
import functools
import math

import jax
import jax.numpy as jnp
from jax import lax
from jax.experimental import pallas as pl
from jax.experimental.pallas import tpu as pltpu
from jax.sharding import PartitionSpec as P

HEAD_DIM = 128
GROUP = 256
N_SEQ = 16
N_HEAD = 4
EPSILON = 1e-06
MASKED = -1e30
SCALE = 1.0 / math.sqrt(HEAD_DIM)
MESH = pl.DeviceIdType.MESH
BF = jnp.bfloat16
F32 = jnp.float32
VMEM_LIMIT = 62 * 1024 * 1024
VM = pl.BlockSpec(memory_space=pltpu.VMEM)
ANY = pl.BlockSpec(memory_space=pl.ANY)


def mm(a, b):
    return lax.dot_general(a, b, (((1,), (0,)), ((), ())), preferred_element_type=F32)


def mm_rows(a, b):
    return lax.dot_general(a, b, (((0,), (0,)), ((), ())), preferred_element_type=F32)


def mm_cols(a, b):
    return lax.dot_general(a, b, (((1,), (1,)), ((), ())), preferred_element_type=F32)


def place():
    s = lax.axis_index("seq")
    return s >> 2, s & 3


def x_copy(d, src, dst, send_sem, recv_sem):
    z, x = place()
    return pltpu.make_async_remote_copy(
        src_ref=src,
        dst_ref=dst,
        send_sem=send_sem,
        recv_sem=recv_sem,
        device_id={"seq": 4 * z + ((x + d) & 3)},
        device_id_type=MESH,
    )


def z_copy(d, src, dst, send_sem, recv_sem):
    z, x = place()
    return pltpu.make_async_remote_copy(
        src_ref=src,
        dst_ref=dst,
        send_sem=send_sem,
        recv_sem=recv_sem,
        device_id={"seq": 4 * ((z + d) & 3) + x},
        device_id_type=MESH,
    )


def greet(with_partner):
    z, x = place()
    h = lax.axis_index("head")
    barrier = pltpu.get_barrier_semaphore()
    for d in range(1, 4):
        for peer in (
            {"seq": 4 * z + ((x + d) & 3)},
            {"seq": 4 * ((z + d) & 3) + x},
            {"head": (h + d) & 3},
        ):
            pl.semaphore_signal(barrier, inc=1, device_id=peer, device_id_type=MESH)
    if with_partner:
        pl.semaphore_signal(
            barrier, inc=1, device_id={"grp": 1 - lax.axis_index("grp")}, device_id_type=MESH
        )


def met(with_partner):
    pl.semaphore_wait(pltpu.get_barrier_semaphore(), 10 if with_partner else 9)


def partner_copy(src, dst, send_sem, recv_sem):
    return pltpu.make_async_remote_copy(
        src_ref=src,
        dst_ref=dst,
        send_sem=send_sem,
        recv_sem=recv_sem,
        device_id={"grp": 1 - lax.axis_index("grp")},
        device_id_type=MESH,
    )


class Swap:
    def __init__(self, source, target, ss, rs):
        self.source, self.target, self.ss, self.rs = source, target, ss, rs
        self.x = place()[1]

    def sending(self, d):
        src = self.source.at[(self.x + d) & 3]
        return x_copy(d, src, self.target.at[self.x], self.ss.at[d - 1], self.rs.at[d - 1])

    def landing(self, d):
        ref = self.target.at[(self.x + 4 - d) & 3]
        return x_copy(d, ref, ref, self.ss.at[d - 1], self.rs.at[d - 1])

    def start(self):
        for d in (2, 1, 3):
            self.sending(d).start()

    def keep(self):
        self.target[self.x] = self.source[self.x]

    def finish(self):
        for d in (1, 3, 2):
            self.landing(d).wait_recv()

    def drain(self):
        for d in (1, 2, 3):
            self.sending(d).wait_send()


class Scatter:
    def __init__(self, blocks, n, slots, sums, last, ss, rs, ss2, rs2):
        self.blocks, self.n = blocks, n
        self.slots, self.sums, self.last = slots, sums, last
        self.ss, self.rs, self.ss2, self.rs2 = ss, rs, ss2, rs2
        self.z, self.x = place()

    def cut(self, half, d):
        rows = pl.ds(half * self.n, self.n)
        if half == 0:
            return self.blocks.at[:, (self.x + d) & 3, rows]
        return self.blocks.at[(self.z + d) & 3, :, rows]

    def first(self, half, d):
        move = x_copy if half == 0 else z_copy
        return move(
            d, self.cut(half, d), self.slots.at[half, d - 1], self.ss.at[half, d - 1], self.rs.at[half, d - 1]
        )

    def second(self, half, d):
        move = z_copy if half == 0 else x_copy
        own = self.z if half == 0 else self.x
        return move(
            d, self.sums.at[half, (own + d) & 3], self.last.at[half, d - 1],
            self.ss2.at[half, d - 1], self.rs2.at[half, d - 1],
        )

    def start(self):
        for d in (2, 1, 3):
            for half in (0, 1):
                self.first(half, d).start()

    def middle(self):
        for half in (0, 1):
            for d in (1, 3, 2):
                self.first(half, d).wait_recv()
            own = self.cut(half, 0)

            def add(k, c):
                total = own[k].astype(F32) + self.slots[half, 0, k].astype(F32)
                total = total + self.slots[half, 1, k].astype(F32) + self.slots[half, 2, k].astype(F32)
                self.sums[half, k] = total.astype(BF)
                return c

            lax.fori_loop(0, 4, add, 0)
            for d in (2, 1, 3):
                self.second(half, d).start()

    def finish(self, half):
        for d in (1, 3, 2):
            self.second(half, d).wait_recv()
        own = self.z if half == 0 else self.x
        total = self.sums[half, own].astype(F32)
        for d in range(3):
            total = total + self.last[half, d].astype(F32)
        return total

    def drain(self):
        for half in (0, 1):
            for d in (1, 2, 3):
                self.first(half, d).wait_send()
                self.second(half, d).wait_send()

    @staticmethod
    def scratch(n):
        dma = pltpu.SemaphoreType.DMA
        return [
            pltpu.VMEM((2, 3, 4, n, 512), BF), pltpu.VMEM((2, 4, n, 512), BF), pltpu.VMEM((2, 3, n, 512), BF),
            dma((2, 3)), dma((2, 3)), dma((2, 3)), dma((2, 3)),
        ]


def head_copy(d, src, dst, ss, rs):
    h = lax.axis_index("head")
    return pltpu.make_async_remote_copy(
        src_ref=src,
        dst_ref=dst,
        send_sem=ss.at[d - 1],
        recv_sem=rs.at[d - 1],
        device_id={"head": lax.rem(h + d, 4)},
        device_id_type=MESH,
    )


class HeadSum:
    def __init__(self, parts, slots, total, ss, rs, ss2, rs2):
        self.parts, self.slots, self.total = parts, slots, total
        self.ss, self.rs, self.ss2, self.rs2 = ss, rs, ss2, rs2
        self.h = lax.axis_index("head")

    def quarter(self, h):
        return pl.ds(pl.multiple_of(h * 64, 64), 64)

    def first(self, d):
        src = self.parts.at[self.quarter(lax.rem(self.h + d, 4))]
        return head_copy(d, src, self.slots.at[d - 1], self.ss, self.rs)

    def second(self, d):
        ref = self.total.at[self.quarter(self.h)]
        return head_copy(d, ref, ref, self.ss2, self.rs2)

    def second_landing(self, d):
        ref = self.total.at[self.quarter(lax.rem(self.h + 4 - d, 4))]
        return head_copy(d, ref, ref, self.ss2, self.rs2)

    def send(self):
        for d in (2, 1, 3):
            self.first(d).start()

    def receive(self):
        total = self.parts[self.quarter(self.h)].astype(F32)
        for d in (1, 3, 2):
            self.first(d).wait_recv()
            total = total + self.slots[d - 1].astype(F32)
        return total

    def share(self, total):
        self.total[self.quarter(self.h)] = total.astype(BF)
        for d in (2, 1, 3):
            self.second(d).start()

    def collect(self):
        for d in (1, 3, 2):
            self.second_landing(d).wait_recv()

    def drain(self):
        for d in (1, 2, 3):
            self.first(d).wait_send()
            self.second(d).wait_send()


def encoder_kernel(
    enc_in, gain, w_in, w_out, w_key, w_value, dec, w_query, w_attn, cot,
    normed, pre_act, activated, enc_out, kv, q_all, dm_all,
    v_in, v_out, v_key, v_value, v_dec, v_query, v_attn, v_cot, load_sem,
    parts, slots, hs1, hr1, hs2, hr2,
    q_send, dm_send, kv_send, qs, qr, ds, dr, ks, kr, zs, zr,
):
    pairs = (
        (w_in, v_in), (w_out, v_out), (dec, v_dec), (w_query, v_query),
        (w_key, v_key), (w_value, v_value), (cot, v_cot), (w_attn, v_attn),
    )
    loads = {id(v): pltpu.make_async_copy(a, v, load_sem.at[i]) for i, (a, v) in enumerate(pairs)}
    greet(False)
    for copy in loads.values():
        copy.start()
    z, x = place()
    encoded = enc_in[...].astype(F32)
    square = jnp.mean(encoded * encoded, axis=1, keepdims=True)
    normed[...] = (encoded * lax.rsqrt(square + EPSILON) * gain[...]).astype(BF)
    loads[id(v_in)].wait()
    for n in range(4):
        cols = pl.ds(n * 256, 256)
        pre = mm(normed[...], v_in[:, cols])
        pre_act[:, cols] = pre
        activated[:, cols] = (pre / (1.0 + jnp.exp(-pre))).astype(BF)
    loads[id(v_out)].wait()
    for n in range(4):
        cols = pl.ds(n * 256, 256)
        parts[:, cols] = mm(activated[...], v_out[:, cols]).astype(BF)
    met(False)
    across = HeadSum(parts, slots, enc_out, hs1, hr1, hs2, hr2)
    across.send()
    q_swap = Swap(q_send, q_all, qs, qr)
    dm_swap = Swap(dm_send, dm_all, ds, dr)
    kv_swap = Swap(kv_send, kv.at[pl.ds(4 * z, 4)], ks, kr)
    loads[id(v_dec)].wait()
    loads[id(v_query)].wait()
    for n in range(2):
        rows = mm(v_dec[...], v_query[:, pl.ds(n * 256, 256)]).astype(BF)
        q_send[2 * n], q_send[2 * n + 1] = rows[:, :128], rows[:, 128:]
    q_swap.start()
    own_rows = across.quarter(across.h)
    across.share(across.receive() + enc_in[own_rows].astype(F32))
    loads[id(v_cot)].wait()
    loads[id(v_attn)].wait()
    for n in range(2):
        rows = mm_cols(v_cot[...], v_attn[pl.ds(n * 256, 256), :]).astype(BF)
        dm_send[2 * n], dm_send[2 * n + 1] = rows[:, :128], rows[:, 128:]
    loads[id(v_key)].wait()
    loads[id(v_value)].wait()
    across.collect()
    for n in range(2):
        for weight, first in ((v_key, 0), (v_value, 128)):
            rows = mm(enc_out[...], weight[:, pl.ds(n * 256, 256)]).astype(BF)
            kv_send[2 * n, :, pl.ds(first, 128)] = rows[:, :128]
            kv_send[2 * n + 1, :, pl.ds(first, 128)] = rows[:, 128:]
    kv_swap.start()
    kv_swap.keep()

    def forward(k, d):
        ref = kv.at[4 * z + ((x + k) & 3)]
        return z_copy(d, ref, ref, zs.at[d - 1, k], zr.at[d - 1, k])

    def arriving(k, d):
        ref = kv.at[4 * ((z + 4 - d) & 3) + ((x + k) & 3)]
        return z_copy(d, ref, ref, zs.at[d - 1, k], zr.at[d - 1, k])

    for d in (2, 1, 3):
        forward(0, d).start()
    dm_swap.start()
    for k in (3, 1, 2):
        kv_swap.landing(4 - k).wait_recv()
        for d in (2, 1, 3):
            forward(k, d).start()
    q_swap.keep()
    dm_swap.keep()
    q_swap.finish()
    dm_swap.finish()
    for k in (0, 3, 1, 2):
        for d in (1, 3, 2):
            arriving(k, d).wait_recv()
    for k in range(4):
        for d in (1, 2, 3):
            forward(k, d).wait_send()
    for swap in (q_swap, dm_swap, kv_swap):
        swap.drain()
    across.drain()


def run_encoder(*args):
    sds = jax.ShapeDtypeStruct
    dma = pltpu.SemaphoreType.DMA
    return pl.pallas_call(
        encoder_kernel,
        out_shape=(
            sds((256, 1024), BF), sds((256, 1024), F32), sds((256, 1024), BF), sds((256, 1024), BF),
            sds((16, 256, 256), BF), sds((4, 256, 128), BF), sds((4, 256, 128), BF),
        ),
        in_specs=[VM, VM] + [ANY] * 8,
        out_specs=(VM,) * 7,
        scratch_shapes=[
            pltpu.VMEM((1024, 1024), BF), pltpu.VMEM((1024, 1024), BF),
            pltpu.VMEM((1024, 512), BF), pltpu.VMEM((1024, 512), BF),
            pltpu.VMEM((256, 4096), BF), pltpu.VMEM((4096, 512), BF),
            pltpu.VMEM((512, 4096), BF), pltpu.VMEM((256, 4096), BF), dma((8,)),
            pltpu.VMEM((256, 1024), BF), pltpu.VMEM((3, 64, 1024), BF),
            dma((3,)), dma((3,)), dma((3,)), dma((3,)),
            pltpu.VMEM((4, 256, 128), BF), pltpu.VMEM((4, 256, 128), BF), pltpu.VMEM((4, 256, 256), BF),
            dma((3,)), dma((3,)), dma((3,)), dma((3,)), dma((3,)), dma((3,)), dma((3, 4)), dma((3, 4)),
        ],
        compiler_params=pltpu.CompilerParams(
            collective_id=0, has_side_effects=True, vmem_limit_bytes=VMEM_LIMIT
        ),
        cost_estimate=pl.CostEstimate(flops=5 * 10**9, bytes_accessed=24 * 2**20, transcendentals=2**18),
        name="encoder_gather",
    )(*args)


def attention_kernel(group_doc, doc_lengths, q_all, dm_all, kv, md, d_kv, scores, acc, d_acc, ends, begins, limits):
    z = lax.axis_index("seq") >> 2
    total = 0
    for j in range(8):
        total = total + doc_lengths[0, j]
        ends[j] = total
    for g in range(N_SEQ):
        doc = group_doc[0, g]
        limits[g] = ends[doc]
        begins[g] = ends[doc] - doc_lengths[0, doc]
    bounds = []
    for b in range(4):
        origin = z * 1024 + b * 256
        lo, hi = 0, 0
        for g in range(N_SEQ):
            lo = lo + jnp.where(limits[g] <= origin, 1, 0)
            hi = hi + jnp.where(begins[g] <= origin + 255, 1, 0)
        bounds.append((origin, lo, hi))
    low, high = bounds[0][1], bounds[3][2]

    def clear(g, c):
        inside = (g >= low) & (g < high)

        @pl.when(inside)
        def _():
            d_acc[g] = jnp.zeros((256, 256), F32)

        @pl.when(jnp.logical_not(inside))
        def _():
            d_kv[g] = jnp.zeros((256, 256), BF)

        return c

    lax.fori_loop(0, N_SEQ, clear, 0)
    for b in range(4):
        origin, lo, hi = bounds[b]
        position = origin + lax.broadcasted_iota(jnp.int32, (256, 1), 0)

        def score(g, m):
            s = mm_cols(q_all[b], kv[g, :, pl.ds(0, 128)]) * SCALE
            seen = (position >= begins[g]) & (position < limits[g])
            s = jnp.where(seen, s, MASKED)
            scores[g] = s
            return jnp.maximum(m, jnp.max(s, axis=1, keepdims=True))

        top = lax.fori_loop(lo, hi, score, jnp.full((256, 1), MASKED, F32))
        acc[...] = jnp.zeros((256, 128), F32)

        def weigh(g, total):
            p = jnp.exp(scores[g] - top)
            scores[g] = p
            acc[...] += mm(p.astype(BF), kv[g, :, pl.ds(128, 128)])
            return total + jnp.sum(p, axis=1, keepdims=True)

        total = lax.fori_loop(lo, hi, weigh, jnp.zeros((256, 1), F32))
        inverse = 1.0 / total
        rows = acc[...] * inverse
        md[b, :, pl.ds(0, 128)] = rows.astype(BF)
        inner = jnp.sum(rows * dm_all[b].astype(F32), axis=1, keepdims=True)
        acc[...] = jnp.zeros((256, 128), F32)

        def back(g, c):
            p = scores[g] * inverse
            dw = mm_cols(dm_all[b], kv[g, :, pl.ds(128, 128)])
            ds = (p * (dw - inner) * SCALE).astype(BF)
            acc[...] += mm(ds, kv[g, :, pl.ds(0, 128)])
            d_acc[g, :, pl.ds(0, 128)] += mm_rows(ds, q_all[b])
            d_acc[g, :, pl.ds(128, 128)] += mm_rows(p.astype(BF), dm_all[b])
            return c

        lax.fori_loop(lo, hi, back, 0)
        md[b, :, pl.ds(128, 128)] = acc[...].astype(BF)

    def settle(g, c):
        d_kv[g] = d_acc[g].astype(BF)
        return c

    lax.fori_loop(low, high, settle, 0)


def run_attention(*args):
    sds = jax.ShapeDtypeStruct
    smem = pl.BlockSpec(memory_space=pltpu.SMEM)
    return pl.pallas_call(
        attention_kernel,
        out_shape=(sds((4, 256, 256), BF), sds((16, 256, 256), BF)),
        in_specs=[smem, smem, VM, VM, VM],
        out_specs=(VM,) * 2,
        scratch_shapes=[
            pltpu.VMEM((16, 256, 256), F32), pltpu.VMEM((256, 128), F32), pltpu.VMEM((16, 256, 256), F32),
            pltpu.SMEM((8,), jnp.int32), pltpu.SMEM((16,), jnp.int32), pltpu.SMEM((16,), jnp.int32),
        ],
        compiler_params=pltpu.CompilerParams(vmem_limit_bytes=VMEM_LIMIT),
        cost_estimate=pl.CostEstimate(flops=2 * 10**9, bytes_accessed=6 * 2**20, transcendentals=2**20),
        name="attention",
    )(*args)


def decoder_kernel(
    d_kv, md, dec, cot, w_attn,
    out, grads, kv_grad,
    v_dec, v_cot, v_attn, load_sem,
    m_all, ms, mr, row_slots, zs, zr, row, kvg, ks, kr, mixed, d_query,
    out_own, out_send, out_recv, os, orr, stage, arrived, ps, pr,
):
    greet(True)
    loads = [
        pltpu.make_async_copy(a, v, load_sem.at[i])
        for i, (a, v) in enumerate(((w_attn, v_attn), (dec, v_dec), (cot, v_cot)))
    ]
    for load in loads:
        load.start()
    met(True)
    z, x = place()
    h = lax.axis_index("head")
    grp = lax.axis_index("grp")
    m_swap = Swap(md, m_all, ms, mr)
    kv_swap = Swap(row, kvg, ks, kr)

    def term(k, d):
        src = d_kv.at[4 * ((z + d) & 3) + ((x + k) & 3)]
        return z_copy(d, src, row_slots.at[d - 1, k], zs.at[d - 1, k], zr.at[d - 1, k])

    m_swap.start()
    for k in (2, 1, 3, 0):
        for d in (2, 1, 3):
            term(k, d).start()
    m_swap.keep()
    m_swap.finish()
    for j in range(4):
        mixed[:, pl.ds(128 * j, 128)] = m_all[j, :, pl.ds(0, 128)]
        d_query[:, pl.ds(128 * j, 128)] = m_all[j, :, pl.ds(128, 128)]

    def out_copy(d):
        return head_copy(d, out_send.at[d - 1], out_recv.at[d - 1], os, orr)

    def part(n, first):
        return pl.ds(pl.multiple_of(first + n * 256, 256), 256)

    loads[0].wait()
    for d in (2, 1, 3):
        first = ((h + d) & 3) * 1024
        for n in range(4):
            out_send[d - 1, :, pl.ds(n * 256, 256)] = mm(mixed[...], v_attn[:, part(n, first)]).astype(BF)
        out_copy(d).start()
    loads[1].wait()
    loads[2].wait()

    def products(u):
        t = (u + 8 * (1 - grp)) & 15
        here = pl.ds(pl.multiple_of(t * 256, 256), 256)
        return mm_rows(v_dec[:, here], d_query[...]), mm_rows(v_cot[:, here], mixed[...])

    def exchange(u):
        pair = pl.ds(2 * u, 2)
        return partner_copy(stage.at[pair], arrived.at[pair], ps.at[u], pr.at[u])

    def far(u, c):
        for which, value in enumerate(products(u)):
            for k in range(2):
                stage[2 * u + k, pl.ds(128 * which, 128)] = value[128 * k : 128 * (k + 1)].astype(BF)
        exchange(u).start()
        return c

    lax.fori_loop(0, 8, far, 0)

    for n in range(4):
        here = part(n, h * 1024)
        out_own[:, pl.ds(n * 256, 256)] = mm(mixed[...], v_attn[:, here]) + v_dec[:, here].astype(F32)

    def near(u, c):
        values = products(u + 8)
        exchange(u).wait_recv()
        for which, value in enumerate(values):
            for k in range(2):
                rows = pl.ds(128 * which, 128)
                both = value[128 * k : 128 * (k + 1)] + arrived[2 * u + k, rows].astype(F32)
                grads[2 * u + k, rows] = both.astype(BF)
        return c

    lax.fori_loop(0, 8, near, 0)

    for k in (2, 1, 3, 0):
        there = (x + k) & 3
        total = d_kv[4 * z + there].astype(F32)
        for d in (1, 3, 2):
            term(k, d).wait_recv()
            total = total + row_slots[d - 1, k].astype(F32)
        row[there] = total.astype(BF)
        if k:
            kv_swap.sending(k).start()
    kv_swap.keep()
    total = out_own[...]
    for d in (1, 3, 2):
        out_copy(d).wait_recv()
        total = total + out_recv[d - 1].astype(F32)
    out[...] = total.astype(BF)
    kv_swap.finish()
    for j in range(4):
        kv_grad[:, pl.ds(128 * j, 128)] = kvg[j, :, pl.ds(0, 128)]
        kv_grad[:, pl.ds(512 + 128 * j, 128)] = kvg[j, :, pl.ds(128, 128)]
    m_swap.drain()
    kv_swap.drain()
    for k in range(4):
        for d in (1, 2, 3):
            term(k, d).wait_send()
    for d in (1, 2, 3):
        out_copy(d).wait_send()

    def sent(u, c):
        exchange(u).wait_send()
        return c

    lax.fori_loop(0, 8, sent, 0)


def run_decoder(*args):
    sds = jax.ShapeDtypeStruct
    dma = pltpu.SemaphoreType.DMA
    return pl.pallas_call(
        decoder_kernel,
        out_shape=(sds((256, 1024), BF), sds((16, 256, 512), BF), sds((256, 1024), BF)),
        in_specs=[VM, VM, ANY, ANY, ANY],
        out_specs=(VM,) * 3,
        scratch_shapes=[
            pltpu.VMEM((256, 4096), BF), pltpu.VMEM((256, 4096), BF), pltpu.VMEM((512, 4096), BF), dma((3,)),
            pltpu.VMEM((4, 256, 256), BF), dma((3,)), dma((3,)),
            pltpu.VMEM((3, 4, 256, 256), BF), dma((3, 4)), dma((3, 4)),
            pltpu.VMEM((4, 256, 256), BF), pltpu.VMEM((4, 256, 256), BF), dma((3,)), dma((3,)),
            pltpu.VMEM((256, 512), BF), pltpu.VMEM((256, 512), BF),
            pltpu.VMEM((256, 1024), F32), pltpu.VMEM((3, 256, 1024), BF), pltpu.VMEM((3, 256, 1024), BF),
            dma((3,)), dma((3,)),
            pltpu.VMEM((16, 256, 512), BF), pltpu.VMEM((16, 256, 512), BF), dma((8,)), dma((8,)),
        ],
        compiler_params=pltpu.CompilerParams(
            collective_id=1, has_side_effects=True, vmem_limit_bytes=VMEM_LIMIT
        ),
        cost_estimate=pl.CostEstimate(flops=4 * 10**9, bytes_accessed=20 * 2**20, transcendentals=0),
        name="decoder_scatter",
    )(*args)


def weights_kernel(
    grads, kv_grad, enc_out, normed, pre_act, activated, w_key, w_value, w_out,
    first, second,
    *scratch,
):
    ring_a, ring_b, ring_c = scratch[0:7], scratch[7:14], scratch[14:21]
    (
        parts, slots, d_enc, hs1, hr1, hs2, hr2, d_pre,
        own_b, stage_b, arrived_b, own_c, stage_c, arrived_c, ps, pr,
    ) = scratch[21:]
    greet(True)
    grp = lax.axis_index("grp")
    k_grad, v_grad = kv_grad.at[:, pl.ds(0, 512)], kv_grad.at[:, pl.ds(512, 512)]
    for n in range(4):
        rows = pl.ds(n * 256, 256)
        part = mm_cols(k_grad[...], w_key[rows, :]) + mm_cols(v_grad[...], w_value[rows, :])
        parts[:, rows] = part.astype(BF)
    met(True)
    across = HeadSum(parts, slots, d_enc, hs1, hr1, hs2, hr2)
    across.send()
    scatter_a = Scatter(grads, 128, *ring_a)
    scatter_a.start()
    far, near = (1 - grp) * 512, grp * 512

    def put(left, right, row, stage, own):
        for base, target in ((far, stage), (near, own)):
            for n in range(2):
                cols = pl.ds(pl.multiple_of(base + n * 256, 256), 256)
                value = mm_rows(left[:, cols], right[...])
                for k in range(8):
                    block = n * 8 + k
                    target[block // 4, block % 4, pl.ds(row, 32)] = value[32 * k : 32 * (k + 1)].astype(BF)

    def add(own, arrived):
        def body(b, c):
            own[b] = (own[b].astype(F32) + arrived[b].astype(F32)).astype(BF)
            return c

        lax.fori_loop(0, 4, body, 0)

    swap_b = partner_copy(stage_b, arrived_b, ps.at[0], pr.at[0])
    put(enc_out, k_grad, 0, stage_b, own_b)
    put(enc_out, v_grad, 32, stage_b, own_b)
    swap_b.start()
    across.share(across.receive())
    swap_b.wait_recv()
    add(own_b, arrived_b)
    scatter_b = Scatter(own_b, 32, *ring_b)
    scatter_b.start()
    across.collect()
    for n in range(4):
        cols = pl.ds(n * 256, 256)
        pre = pre_act[:, cols]
        sig = 1.0 / (1.0 + jnp.exp(-pre))
        slope = sig * (1.0 + pre * (1.0 - sig))
        d_pre[:, cols] = (mm_cols(d_enc[...], w_out[cols, :]) * slope).astype(BF)
    halves = [pl.ds(64 * which, 64) for which in range(2)]
    swap_c = [
        partner_copy(stage_c.at[:, :, r], arrived_c.at[:, :, r], ps.at[1 + i], pr.at[1 + i])
        for i, r in enumerate(halves)
    ]
    for n in range(2):
        put(d_enc, activated.at[:, pl.ds(512 * n, 512)], 64 + 32 * n, stage_c, own_c)
    swap_c[1].start()
    for n in range(2):
        put(normed, d_pre.at[:, pl.ds(512 * n, 512)], 32 * n, stage_c, own_c)
    swap_c[0].start()
    for copy in (swap_c[1], swap_c[0]):
        copy.wait_recv()
    add(own_c, arrived_c)
    scatter_c = Scatter(own_c, 64, *ring_c)
    scatter_c.start()
    scatter_a.middle()
    scatter_b.middle()
    for half in range(2):
        first[pl.ds(128 * half, 128)] = scatter_a.finish(half)
    for half in range(2):
        second[pl.ds(32 * half, 32)] = scatter_b.finish(half)
    scatter_c.middle()
    scatter_a.drain()
    scatter_b.drain()
    across.drain()
    for copy in (swap_b, *swap_c):
        copy.wait_send()
    for half in range(2):
        second[pl.ds(64 + 64 * half, 64)] = scatter_c.finish(half)
    scatter_c.drain()


def run_weights(*args):
    sds = jax.ShapeDtypeStruct
    dma = pltpu.SemaphoreType.DMA
    return pl.pallas_call(
        weights_kernel,
        out_shape=(sds((256, 512), F32), sds((192, 512), F32)),
        in_specs=[VM] * 9,
        out_specs=(VM,) * 2,
        scratch_shapes=[
            *Scatter.scratch(128), *Scatter.scratch(32), *Scatter.scratch(64),
            pltpu.VMEM((256, 1024), BF), pltpu.VMEM((3, 64, 1024), BF), pltpu.VMEM((256, 1024), BF),
            dma((3,)), dma((3,)), dma((3,)), dma((3,)),
            pltpu.VMEM((256, 1024), BF),
            *[pltpu.VMEM((4, 4, 64, 512), BF)] * 3, *[pltpu.VMEM((4, 4, 128, 512), BF)] * 3,
            dma((3,)), dma((3,)),
        ],
        compiler_params=pltpu.CompilerParams(
            collective_id=2, has_side_effects=True, vmem_limit_bytes=VMEM_LIMIT
        ),
        cost_estimate=pl.CostEstimate(flops=3 * 10**9, bytes_accessed=16 * 2**20, transcendentals=2**18),
        name="weights_scatter",
    )(*args)


def unpack_kernel(first, second, out_in, out, g_query, g_key, g_value, g_attn, g_in, g_out):
    out[...] = out_in[...]
    g_query[...] = first[pl.ds(0, 128)]
    g_attn[...] = first[pl.ds(128, 128)].T
    g_key[...] = second[pl.ds(0, 32)]
    g_value[...] = second[pl.ds(32, 32)]
    for n in range(2):
        cols = pl.ds(512 * n, 512)
        g_in[:, cols] = second[pl.ds(64 + 32 * n, 32)]
        g_out[cols, :] = second[pl.ds(128 + 32 * n, 32)].T


def run_unpack(first, second, out):
    sds = jax.ShapeDtypeStruct
    return pl.pallas_call(
        unpack_kernel,
        out_shape=(
            sds((256, 1024), BF), sds((128, 512), F32), sds((32, 512), F32), sds((32, 512), F32),
            sds((512, 128), F32), sds((32, 1024), F32), sds((1024, 32), F32),
        ),
        in_specs=[VM] * 3,
        out_specs=(VM,) * 7,
        name="unpack",
    )(first, second, out)


def shards(
    enc_in, enc_gain, w_in, w_out, w_key, w_value, dec_in, w_query, w_attn_out, cotangent, group_doc, doc_lengths,
):
    normed, pre_act, activated, enc_out, kv, q_all, dm_all = run_encoder(
        enc_in[0], enc_gain[None, :], w_in, w_out, w_key, w_value, dec_in[0], w_query, w_attn_out, cotangent[0]
    )
    md, d_kv = run_attention(group_doc, doc_lengths, q_all, dm_all, kv)
    out, grads, kv_grad = run_decoder(d_kv, md, dec_in[0], cotangent[0], w_attn_out)
    first, second = run_weights(
        grads.reshape(4, 4, 256, 512), kv_grad, enc_out, normed, pre_act, activated, w_key, w_value, w_out
    )
    out, g_query, g_key, g_value, g_attn, g_in, g_out = run_unpack(first, second, out)
    return (out[None], g_query, g_key, g_value, g_attn, g_in, g_out)


def solution(mesh):
    placed = (
        P("grp", "seq", None),
        P(),
        P(None, "head"),
        P("head", None),
        P(None, "head"),
        P(None, "head"),
        P("grp", "seq", None),
        P(None, "head"),
        P("head", None),
        P("grp", "seq", None),
        P("grp", None),
        P("grp", None),
    )
    return jax.shard_map(
        shards,
        mesh=mesh,
        in_specs=placed,
        out_specs=(
            P("grp", "seq", "head"),
            P(("grp", "seq"), "head"),
            P(("grp", "seq"), "head"),
            P(("grp", "seq"), "head"),
            P("head", ("grp", "seq")),
            P(("grp", "seq"), "head"),
            P("head", ("grp", "seq")),
        ),
        check_vma=False,
    )
```

```python
import functools
import math

import jax
import jax.numpy as jnp
from jax import lax
from jax.experimental import pallas as pl
from jax.experimental.pallas import tpu as pltpu
from jax.sharding import PartitionSpec as P

HEAD_DIM = 128
GROUP = 256
N_SEQ = 16
N_HEAD = 4
EPSILON = 1e-06
MASKED = -1e30
SCALE = 1.0 / math.sqrt(HEAD_DIM)
MESH = pl.DeviceIdType.MESH
BF = jnp.bfloat16
F32 = jnp.float32
VMEM_LIMIT = 62 * 1024 * 1024
VM = pl.BlockSpec(memory_space=pltpu.VMEM)
ANY = pl.BlockSpec(memory_space=pl.ANY)


def mm(a, b):
    return lax.dot_general(a, b, (((1,), (0,)), ((), ())), preferred_element_type=F32)


def mm_rows(a, b):
    return lax.dot_general(a, b, (((0,), (0,)), ((), ())), preferred_element_type=F32)


def mm_cols(a, b):
    return lax.dot_general(a, b, (((1,), (1,)), ((), ())), preferred_element_type=F32)


def place():
    s = lax.axis_index("seq")
    return s >> 2, s & 3


def device_at(along, across):
    grp = lax.axis_index("grp")
    return (4 - 3 * grp) * along + (1 + 3 * grp) * across


def role():
    z, x = place()
    grp = lax.axis_index("grp")
    return (1 - grp) * z + grp * x, (1 - grp) * x + grp * z


def seq_copy(peer, src, dst, send_sem, recv_sem):
    return pltpu.make_async_remote_copy(
        src_ref=src,
        dst_ref=dst,
        send_sem=send_sem,
        recv_sem=recv_sem,
        device_id={"seq": peer},
        device_id_type=MESH,
    )


def x_copy(d, *rest):
    z, x = place()
    return seq_copy(4 * z + ((x + d) & 3), *rest)


def z_copy(d, *rest):
    z, x = place()
    return seq_copy(4 * ((z + d) & 3) + x, *rest)


def across_copy(d, *rest):
    along, across = role()
    return seq_copy(device_at(along, (across + d) & 3), *rest)


def along_copy(d, *rest):
    along, across = role()
    return seq_copy(device_at((along + d) & 3, across), *rest)


def greet(with_partner):
    z, x = place()
    h = lax.axis_index("head")
    barrier = pltpu.get_barrier_semaphore()
    for d in range(1, 4):
        for peer in (
            {"seq": 4 * z + ((x + d) & 3)},
            {"seq": 4 * ((z + d) & 3) + x},
            {"head": (h + d) & 3},
        ):
            pl.semaphore_signal(barrier, inc=1, device_id=peer, device_id_type=MESH)
    if with_partner:
        pl.semaphore_signal(
            barrier, inc=1, device_id={"grp": 1 - lax.axis_index("grp")}, device_id_type=MESH
        )


def met(with_partner):
    pl.semaphore_wait(pltpu.get_barrier_semaphore(), 10 if with_partner else 9)


def partner_copy(src, dst, send_sem, recv_sem):
    return pltpu.make_async_remote_copy(
        src_ref=src,
        dst_ref=dst,
        send_sem=send_sem,
        recv_sem=recv_sem,
        device_id={"grp": 1 - lax.axis_index("grp")},
        device_id_type=MESH,
    )


class Swap:
    def __init__(self, source, target, ss, rs):
        self.source, self.target, self.ss, self.rs = source, target, ss, rs
        self.x = role()[1]

    def sending(self, d):
        src = self.source.at[(self.x + d) & 3]
        return across_copy(d, src, self.target.at[self.x], self.ss.at[d - 1], self.rs.at[d - 1])

    def landing(self, d):
        ref = self.target.at[(self.x + 4 - d) & 3]
        return across_copy(d, ref, ref, self.ss.at[d - 1], self.rs.at[d - 1])

    def start(self):
        for d in (2, 1, 3):
            self.sending(d).start()

    def keep(self):
        self.target[self.x] = self.source[self.x]

    def finish(self):
        for d in (1, 3, 2):
            self.landing(d).wait_recv()

    def drain(self):
        for d in (1, 2, 3):
            self.sending(d).wait_send()


class Scatter:
    def __init__(self, blocks, n, slots, sums, last, ss, rs, ss2, rs2):
        self.blocks, self.n = blocks, n
        self.slots, self.sums, self.last = slots, sums, last
        self.ss, self.rs, self.ss2, self.rs2 = ss, rs, ss2, rs2
        self.z, self.x = place()

    def cut(self, half, d, chunk):
        rows = pl.ds(half * self.n, self.n)
        two = pl.ds(2 * chunk, 2)
        if half == 0:
            return self.blocks.at[two, (self.x + d) & 3, rows]
        return self.blocks.at[(self.z + d) & 3, two, rows]

    def first(self, half, d, chunk):
        move = x_copy if half == 0 else z_copy
        return move(
            d, self.cut(half, d, chunk), self.slots.at[half, d - 1, pl.ds(2 * chunk, 2)],
            self.ss.at[half, d - 1, chunk], self.rs.at[half, d - 1, chunk],
        )

    def second(self, half, d):
        move = z_copy if half == 0 else x_copy
        own = self.z if half == 0 else self.x
        return move(
            d, self.sums.at[half, (own + d) & 3], self.last.at[half, d - 1],
            self.ss2.at[half, d - 1], self.rs2.at[half, d - 1],
        )

    def start(self, half, chunk):
        for d in (2, 1, 3):
            self.first(half, d, chunk).start()

    def start_all(self):
        for chunk in (0, 1):
            for half in (0, 1):
                self.start(half, chunk)

    def middle(self, halves=(0, 1)):
        for half in halves:
            for chunk in (0, 1):
                for d in (1, 3, 2):
                    self.first(half, d, chunk).wait_recv()
                own = self.cut(half, 0, chunk)
                for k in range(2):
                    total = own[k].astype(F32)
                    for d in range(3):
                        total = total + self.slots[half, d, 2 * chunk + k].astype(F32)
                    self.sums[half, 2 * chunk + k] = total.astype(BF)
            for d in (2, 1, 3):
                self.second(half, d).start()

    def finish(self, half):
        for d in (1, 3, 2):
            self.second(half, d).wait_recv()
        own = self.z if half == 0 else self.x
        total = self.sums[half, own].astype(F32)
        for d in range(3):
            total = total + self.last[half, d].astype(F32)
        return total

    def drain(self):
        for half in (0, 1):
            for d in (1, 2, 3):
                for chunk in (0, 1):
                    self.first(half, d, chunk).wait_send()
                self.second(half, d).wait_send()

    @staticmethod
    def scratch(n):
        dma = pltpu.SemaphoreType.DMA
        return [
            pltpu.VMEM((2, 3, 4, n, 512), BF), pltpu.VMEM((2, 4, n, 512), BF), pltpu.VMEM((2, 3, n, 512), BF),
            dma((2, 3, 2)), dma((2, 3, 2)), dma((2, 3)), dma((2, 3)),
        ]


def head_copy(d, src, dst, ss, rs):
    h = lax.axis_index("head")
    return pltpu.make_async_remote_copy(
        src_ref=src,
        dst_ref=dst,
        send_sem=ss.at[d - 1],
        recv_sem=rs.at[d - 1],
        device_id={"head": lax.rem(h + d, 4)},
        device_id_type=MESH,
    )


class HeadSum:
    def __init__(self, parts, slots, total, ss, rs, ss2, rs2):
        self.parts, self.slots, self.total = parts, slots, total
        self.ss, self.rs, self.ss2, self.rs2 = ss, rs, ss2, rs2
        self.h = lax.axis_index("head")

    def quarter(self, h):
        return pl.ds(pl.multiple_of(h * 64, 64), 64)

    def first(self, d):
        src = self.parts.at[self.quarter(lax.rem(self.h + d, 4))]
        return head_copy(d, src, self.slots.at[d - 1], self.ss, self.rs)

    def second(self, d):
        ref = self.total.at[self.quarter(self.h)]
        return head_copy(d, ref, ref, self.ss2, self.rs2)

    def second_landing(self, d):
        ref = self.total.at[self.quarter(lax.rem(self.h + 4 - d, 4))]
        return head_copy(d, ref, ref, self.ss2, self.rs2)

    def send(self):
        for d in (2, 1, 3):
            self.first(d).start()

    def receive(self):
        total = self.parts[self.quarter(self.h)].astype(F32)
        for d in (1, 3, 2):
            self.first(d).wait_recv()
            total = total + self.slots[d - 1].astype(F32)
        return total

    def share(self, total):
        self.total[self.quarter(self.h)] = total.astype(BF)
        for d in (2, 1, 3):
            self.second(d).start()

    def collect(self):
        for d in (1, 3, 2):
            self.second_landing(d).wait_recv()

    def drain(self):
        for d in (1, 2, 3):
            self.first(d).wait_send()
            self.second(d).wait_send()


def encoder_kernel(
    enc_in, gain, w_in, w_out, w_key, w_value, dec, w_query, w_attn, cot,
    normed, pre_act, activated, enc_out, kv, q_all, dm_all,
    v_in, v_out, v_key, v_value, v_dec, v_query, v_attn, v_cot, load_sem,
    parts, slots, hs1, hr1, hs2, hr2,
    q_send, dm_send, kv_send, qs, qr, ds, dr, ks, kr, zs, zr,
):
    pairs = (
        (w_in, v_in), (w_out, v_out), (dec, v_dec), (w_query, v_query),
        (w_key, v_key), (w_value, v_value), (cot, v_cot), (w_attn, v_attn),
    )
    loads = {id(v): pltpu.make_async_copy(a, v, load_sem.at[i]) for i, (a, v) in enumerate(pairs)}
    greet(False)
    for copy in loads.values():
        copy.start()
    along, across_at = role()
    encoded = enc_in[...].astype(F32)
    square = jnp.mean(encoded * encoded, axis=1, keepdims=True)
    normed[...] = (encoded * lax.rsqrt(square + EPSILON) * gain[...]).astype(BF)
    loads[id(v_in)].wait()
    for n in range(4):
        cols = pl.ds(n * 256, 256)
        pre = mm(normed[...], v_in[:, cols])
        pre_act[:, cols] = pre
        activated[:, cols] = (pre / (1.0 + jnp.exp(-pre))).astype(BF)
    loads[id(v_out)].wait()
    for n in range(4):
        cols = pl.ds(n * 256, 256)
        parts[:, cols] = mm(activated[...], v_out[:, cols]).astype(BF)
    met(False)
    across = HeadSum(parts, slots, enc_out, hs1, hr1, hs2, hr2)
    across.send()
    q_swap = Swap(q_send, q_all, qs, qr)
    dm_swap = Swap(dm_send, dm_all, ds, dr)
    kv_swap = Swap(kv_send, kv.at[pl.ds(4 * along, 4)], ks, kr)
    loads[id(v_dec)].wait()
    loads[id(v_query)].wait()
    for n in range(2):
        rows = mm(v_dec[...], v_query[:, pl.ds(n * 256, 256)]).astype(BF)
        q_send[2 * n], q_send[2 * n + 1] = rows[:, :128], rows[:, 128:]
    q_swap.start()
    own_rows = across.quarter(across.h)
    across.share(across.receive() + enc_in[own_rows].astype(F32))
    loads[id(v_cot)].wait()
    loads[id(v_attn)].wait()
    for n in range(2):
        rows = mm_cols(v_cot[...], v_attn[pl.ds(n * 256, 256), :]).astype(BF)
        dm_send[2 * n], dm_send[2 * n + 1] = rows[:, :128], rows[:, 128:]
    loads[id(v_key)].wait()
    loads[id(v_value)].wait()
    across.collect()
    for n in range(2):
        for weight, first in ((v_key, 0), (v_value, 128)):
            rows = mm(enc_out[...], weight[:, pl.ds(n * 256, 256)]).astype(BF)
            kv_send[2 * n, :, pl.ds(first, 128)] = rows[:, :128]
            kv_send[2 * n + 1, :, pl.ds(first, 128)] = rows[:, 128:]
    kv_swap.start()
    kv_swap.keep()

    def forward(k, d):
        ref = kv.at[4 * along + ((across_at + k) & 3)]
        return along_copy(d, ref, ref, zs.at[d - 1, k], zr.at[d - 1, k])

    def arriving(k, d):
        ref = kv.at[4 * ((along + 4 - d) & 3) + ((across_at + k) & 3)]
        return along_copy(d, ref, ref, zs.at[d - 1, k], zr.at[d - 1, k])

    for d in (2, 1, 3):
        forward(0, d).start()
    dm_swap.start()
    for k in (3, 1, 2):
        kv_swap.landing(4 - k).wait_recv()
        for d in (2, 1, 3):
            forward(k, d).start()
    q_swap.keep()
    dm_swap.keep()
    q_swap.finish()
    dm_swap.finish()
    for k in (0, 3, 1, 2):
        for d in (1, 3, 2):
            arriving(k, d).wait_recv()
    for k in range(4):
        for d in (1, 2, 3):
            forward(k, d).wait_send()
    for swap in (q_swap, dm_swap, kv_swap):
        swap.drain()
    across.drain()


def run_encoder(*args):
    sds = jax.ShapeDtypeStruct
    dma = pltpu.SemaphoreType.DMA
    return pl.pallas_call(
        encoder_kernel,
        out_shape=(
            sds((256, 1024), BF), sds((256, 1024), F32), sds((256, 1024), BF), sds((256, 1024), BF),
            sds((16, 256, 256), BF), sds((4, 256, 128), BF), sds((4, 256, 128), BF),
        ),
        in_specs=[VM, VM] + [ANY] * 8,
        out_specs=(VM,) * 7,
        scratch_shapes=[
            pltpu.VMEM((1024, 1024), BF), pltpu.VMEM((1024, 1024), BF),
            pltpu.VMEM((1024, 512), BF), pltpu.VMEM((1024, 512), BF),
            pltpu.VMEM((256, 4096), BF), pltpu.VMEM((4096, 512), BF),
            pltpu.VMEM((512, 4096), BF), pltpu.VMEM((256, 4096), BF), dma((8,)),
            pltpu.VMEM((256, 1024), BF), pltpu.VMEM((3, 64, 1024), BF),
            dma((3,)), dma((3,)), dma((3,)), dma((3,)),
            pltpu.VMEM((4, 256, 128), BF), pltpu.VMEM((4, 256, 128), BF), pltpu.VMEM((4, 256, 256), BF),
            dma((3,)), dma((3,)), dma((3,)), dma((3,)), dma((3,)), dma((3,)), dma((3, 4)), dma((3, 4)),
        ],
        compiler_params=pltpu.CompilerParams(
            collective_id=0, has_side_effects=True, vmem_limit_bytes=VMEM_LIMIT
        ),
        cost_estimate=pl.CostEstimate(flops=5 * 10**9, bytes_accessed=24 * 2**20, transcendentals=2**18),
        name="encoder_gather",
    )(*args)


def attention_kernel(group_doc, doc_lengths, q_all, dm_all, kv, md, d_kv, scores, acc, d_acc, ends, begins, limits):
    along = role()[0]
    total = 0
    for j in range(8):
        total = total + doc_lengths[0, j]
        ends[j] = total
    for g in range(N_SEQ):
        doc = group_doc[0, g]
        limits[g] = ends[doc]
        begins[g] = ends[doc] - doc_lengths[0, doc]
    bounds = []
    for b in range(4):
        origin = device_at(along, b) * 256
        lo, hi = 0, 0
        for g in range(N_SEQ):
            lo = lo + jnp.where(limits[g] <= origin, 1, 0)
            hi = hi + jnp.where(begins[g] <= origin + 255, 1, 0)
        bounds.append((origin, lo, hi))
    low, high = bounds[0][1], bounds[3][2]

    def at(g):
        return device_at(g >> 2, g & 3)

    def clear(g, c):
        inside = (g >= low) & (g < high)

        @pl.when(inside)
        def _():
            d_acc[g] = jnp.zeros((256, 256), F32)

        @pl.when(jnp.logical_not(inside))
        def _():
            d_kv[at(g)] = jnp.zeros((256, 256), BF)

        return c

    lax.fori_loop(0, N_SEQ, clear, 0)
    for b in range(4):
        origin, lo, hi = bounds[b]
        position = origin + lax.broadcasted_iota(jnp.int32, (256, 1), 0)

        def score(g, m):
            s = mm_cols(q_all[b], kv[at(g), :, pl.ds(0, 128)]) * SCALE
            seen = (position >= begins[g]) & (position < limits[g])
            s = jnp.where(seen, s, MASKED)
            scores[g] = s
            return jnp.maximum(m, jnp.max(s, axis=1, keepdims=True))

        top = lax.fori_loop(lo, hi, score, jnp.full((256, 1), MASKED, F32))
        acc[...] = jnp.zeros((256, 128), F32)

        def weigh(g, total):
            p = jnp.exp(scores[g] - top)
            scores[g] = p
            acc[...] += mm(p.astype(BF), kv[at(g), :, pl.ds(128, 128)])
            return total + jnp.sum(p, axis=1, keepdims=True)

        total = lax.fori_loop(lo, hi, weigh, jnp.zeros((256, 1), F32))
        inverse = 1.0 / total
        rows = acc[...] * inverse
        md[b, :, pl.ds(0, 128)] = rows.astype(BF)
        inner = jnp.sum(rows * dm_all[b].astype(F32), axis=1, keepdims=True)
        acc[...] = jnp.zeros((256, 128), F32)

        def back(g, c):
            p = scores[g] * inverse
            dw = mm_cols(dm_all[b], kv[at(g), :, pl.ds(128, 128)])
            ds = (p * (dw - inner) * SCALE).astype(BF)
            acc[...] += mm(ds, kv[at(g), :, pl.ds(0, 128)])
            d_acc[g, :, pl.ds(0, 128)] += mm_rows(ds, q_all[b])
            d_acc[g, :, pl.ds(128, 128)] += mm_rows(p.astype(BF), dm_all[b])
            return c

        lax.fori_loop(lo, hi, back, 0)
        md[b, :, pl.ds(128, 128)] = acc[...].astype(BF)

    def settle(g, c):
        d_kv[at(g)] = d_acc[g].astype(BF)
        return c

    lax.fori_loop(low, high, settle, 0)


def run_attention(*args):
    sds = jax.ShapeDtypeStruct
    smem = pl.BlockSpec(memory_space=pltpu.SMEM)
    return pl.pallas_call(
        attention_kernel,
        out_shape=(sds((4, 256, 256), BF), sds((16, 256, 256), BF)),
        in_specs=[smem, smem, VM, VM, VM],
        out_specs=(VM,) * 2,
        scratch_shapes=[
            pltpu.VMEM((16, 256, 256), F32), pltpu.VMEM((256, 128), F32), pltpu.VMEM((16, 256, 256), F32),
            pltpu.SMEM((8,), jnp.int32), pltpu.SMEM((16,), jnp.int32), pltpu.SMEM((16,), jnp.int32),
        ],
        compiler_params=pltpu.CompilerParams(vmem_limit_bytes=VMEM_LIMIT),
        cost_estimate=pl.CostEstimate(flops=2 * 10**9, bytes_accessed=6 * 2**20, transcendentals=2**20),
        name="attention",
    )(*args)


def decoder_kernel(
    d_kv, md, dec, cot, w_attn, w_key, w_value, w_out, enc_out, normed, activated, pre_act,
    out, first, second,
    *scratch,
):
    ring_a, ring_b, ring_c = scratch[0:7], scratch[7:14], scratch[14:21]
    v_dec, v_cot, v_attn, v_key, v_value, v_out, v_enc, v_normed, v_act, v_pre, load_sem = scratch[21:32]
    (
        m_all, ms, mr, row_slots, zs, zr, row, kvg, ks, kr, mixed, d_query,
        out_own, out_send, out_recv, os, orr, stage, arrived, ps, pr,
    ) = scratch[32:53]
    (
        k_grad, v_grad, parts, slots, d_enc, hs1, hr1, hs2, hr2, d_pre,
        own_b, stage_b, arrived_b, own_c, stage_c, arrived_c, cs, cr,
    ) = scratch[53:]
    greet(True)
    loads = [
        pltpu.make_async_copy(a, v, load_sem.at[i])
        for i, (a, v) in enumerate((
            (w_attn, v_attn), (dec, v_dec), (cot, v_cot), (w_key, v_key), (w_value, v_value),
            (enc_out, v_enc), (w_out, v_out), (pre_act, v_pre), (activated, v_act), (normed, v_normed),
        ))
    ]
    for load in loads:
        load.start()
    met(True)
    along, across_at = role()
    h = lax.axis_index("head")
    grp = lax.axis_index("grp")
    m_swap = Swap(md, m_all, ms, mr)
    kv_swap = Swap(row, kvg, ks, kr)

    def term(k, d):
        src = d_kv.at[4 * ((along + d) & 3) + ((across_at + k) & 3)]
        return along_copy(d, src, row_slots.at[d - 1, k], zs.at[d - 1, k], zr.at[d - 1, k])

    m_swap.start()
    for k in (2, 1, 3, 0):
        for d in (2, 1, 3):
            term(k, d).start()
    m_swap.keep()
    m_swap.finish()
    for j in range(4):
        mixed[:, pl.ds(128 * j, 128)] = m_all[j, :, pl.ds(0, 128)]
        d_query[:, pl.ds(128 * j, 128)] = m_all[j, :, pl.ds(128, 128)]

    def out_copy(d):
        return head_copy(d, out_send.at[d - 1], out_recv.at[d - 1], os, orr)

    def part(n, start):
        return pl.ds(pl.multiple_of(start + n * 256, 256), 256)

    loads[0].wait()
    for d in (2, 1, 3):
        start = ((h + d) & 3) * 1024
        for n in range(4):
            out_send[d - 1, :, pl.ds(n * 256, 256)] = mm(mixed[...], v_attn[:, part(n, start)]).astype(BF)
        out_copy(d).start()
    loads[1].wait()
    loads[2].wait()

    def products(u):
        t = (u + 8 * (1 - grp)) & 15
        here = pl.ds(pl.multiple_of(t * 256, 256), 256)
        return mm_rows(v_dec[:, here], d_query[...]), mm_rows(v_cot[:, here], mixed[...])

    def exchange(u):
        place_u = (u >> 1, pl.ds(2 * (u & 1), 2))
        return partner_copy(stage.at[place_u], arrived.at[place_u], ps.at[u], pr.at[u])

    def far(u, c):
        for which, value in enumerate(products(u)):
            for k in range(2):
                stage[u >> 1, 2 * (u & 1) + k, pl.ds(128 * which, 128)] = value[128 * k : 128 * (k + 1)].astype(BF)
        exchange(u).start()
        return c

    lax.fori_loop(0, 8, far, 0)
    for k in (2, 1, 3, 0):
        there = (across_at + k) & 3
        total = d_kv[4 * along + there].astype(F32)
        for d in (1, 3, 2):
            term(k, d).wait_recv()
            total = total + row_slots[d - 1, k].astype(F32)
        row[there] = total.astype(BF)
        if k:
            kv_swap.sending(k).start()
    kv_swap.keep()

    def near(u, c):
        values = products(u + 8)
        exchange(u).wait_recv()
        for which, value in enumerate(values):
            for k in range(2):
                rows = pl.ds(128 * which, 128)
                block = 2 * (u & 1) + k
                both = value[128 * k : 128 * (k + 1)] + arrived[u >> 1, block, rows].astype(F32)
                arrived[u >> 1, block, rows] = both.astype(BF)
        return c

    lax.fori_loop(0, 8, near, 0)
    scatter_a = Scatter(arrived, 128, *ring_a)
    scatter_a.start_all()
    kv_swap.finish()
    for j in range(4):
        k_grad[:, pl.ds(128 * j, 128)] = kvg[j, :, pl.ds(0, 128)]
        v_grad[:, pl.ds(128 * j, 128)] = kvg[j, :, pl.ds(128, 128)]
    loads[3].wait()
    loads[4].wait()
    for n in range(4):
        rows = pl.ds(n * 256, 256)
        value = mm_cols(k_grad[...], v_key[rows, :]) + mm_cols(v_grad[...], v_value[rows, :])
        parts[:, rows] = value.astype(BF)
    total_d = HeadSum(parts, slots, d_enc, hs1, hr1, hs2, hr2)
    total_d.send()

    for n in range(4):
        here = part(n, h * 1024)
        out_own[:, pl.ds(n * 256, 256)] = mm(mixed[...], v_attn[:, here]) + v_dec[:, here].astype(F32)
    far_from, near_from = (1 - grp) * 512, grp * 512

    def put(left, right, row_at, far_to, near_to):
        for base, target in ((far_from, far_to), (near_from, near_to)):
            for n in range(2):
                cols = part(n, base)
                value = mm_rows(left[:, cols], right[...])
                for k in range(8):
                    block = n * 8 + k
                    target[block // 4, block % 4, pl.ds(row_at, 32)] = value[32 * k : 32 * (k + 1)].astype(BF)

    def add(own, more):
        def body(b, c):
            own[b] = (own[b].astype(F32) + more[b].astype(F32)).astype(BF)
            return c

        lax.fori_loop(0, 4, body, 0)

    loads[5].wait()
    swap_b = partner_copy(stage_b, arrived_b, cs.at[0], cr.at[0])
    put(v_enc, k_grad, 0, stage_b, own_b)
    put(v_enc, v_grad, 32, stage_b, own_b)
    swap_b.start()
    total_d.share(total_d.receive())
    swap_b.wait_recv()
    add(own_b, arrived_b)
    scatter_b = Scatter(own_b, 32, *ring_b)
    scatter_b.start_all()
    total = out_own[...]
    for d in (1, 3, 2):
        out_copy(d).wait_recv()
        total = total + out_recv[d - 1].astype(F32)
    out[...] = total.astype(BF)
    for load in loads[6:]:
        load.wait()
    total_d.collect()
    for n in range(4):
        cols = pl.ds(n * 256, 256)
        pre = v_pre[:, cols]
        sig = 1.0 / (1.0 + jnp.exp(-pre))
        slope = sig * (1.0 + pre * (1.0 - sig))
        d_pre[:, cols] = (mm_cols(d_enc[...], v_out[cols, :]) * slope).astype(BF)
    halves = [pl.ds(64 * which, 64) for which in range(2)]
    swap_c = [
        partner_copy(stage_c.at[:, :, r], arrived_c.at[:, :, r], cs.at[1 + i], cr.at[1 + i])
        for i, r in enumerate(halves)
    ]
    for n in range(2):
        put(d_enc, v_act.at[:, pl.ds(512 * n, 512)], 64 + 32 * n, stage_c, own_c)
    swap_c[1].start()
    for n in range(2):
        put(v_normed, d_pre.at[:, pl.ds(512 * n, 512)], 32 * n, stage_c, own_c)
    swap_c[0].start()
    scatter_a.middle()
    for copy in (swap_c[1], swap_c[0]):
        copy.wait_recv()
    add(own_c, arrived_c)
    scatter_c = Scatter(own_c, 64, *ring_c)
    scatter_c.start_all()
    scatter_b.middle()
    for half in range(2):
        first[pl.ds(128 * half, 128)] = scatter_a.finish(half)
    for half in range(2):
        second[pl.ds(32 * half, 32)] = scatter_b.finish(half)
    scatter_c.middle()
    m_swap.drain()
    kv_swap.drain()
    for k in range(4):
        for d in (1, 2, 3):
            term(k, d).wait_send()
    for d in (1, 2, 3):
        out_copy(d).wait_send()

    def sent(u, c):
        exchange(u).wait_send()
        return c

    lax.fori_loop(0, 8, sent, 0)
    scatter_a.drain()
    scatter_b.drain()
    total_d.drain()
    for copy in (swap_b, *swap_c):
        copy.wait_send()
    for half in range(2):
        second[pl.ds(64 + 64 * half, 64)] = scatter_c.finish(half)
    scatter_c.drain()


def run_decoder(*args):
    sds = jax.ShapeDtypeStruct
    dma = pltpu.SemaphoreType.DMA
    return pl.pallas_call(
        decoder_kernel,
        out_shape=(sds((256, 1024), BF), sds((256, 512), F32), sds((192, 512), F32)),
        in_specs=[VM, VM] + [ANY] * 10,
        out_specs=(VM,) * 3,
        scratch_shapes=[
            *Scatter.scratch(128), *Scatter.scratch(32), *Scatter.scratch(64),
            pltpu.VMEM((256, 4096), BF), pltpu.VMEM((256, 4096), BF), pltpu.VMEM((512, 4096), BF),
            pltpu.VMEM((1024, 512), BF), pltpu.VMEM((1024, 512), BF), pltpu.VMEM((1024, 1024), BF),
            pltpu.VMEM((256, 1024), BF), pltpu.VMEM((256, 1024), BF), pltpu.VMEM((256, 1024), BF),
            pltpu.VMEM((256, 1024), F32), dma((10,)),
            pltpu.VMEM((4, 256, 256), BF), dma((3,)), dma((3,)),
            pltpu.VMEM((3, 4, 256, 256), BF), dma((3, 4)), dma((3, 4)),
            pltpu.VMEM((4, 256, 256), BF), pltpu.VMEM((4, 256, 256), BF), dma((3,)), dma((3,)),
            pltpu.VMEM((256, 512), BF), pltpu.VMEM((256, 512), BF),
            pltpu.VMEM((256, 1024), F32), pltpu.VMEM((3, 256, 1024), BF), pltpu.VMEM((3, 256, 1024), BF),
            dma((3,)), dma((3,)),
            pltpu.VMEM((4, 4, 256, 512), BF), pltpu.VMEM((4, 4, 256, 512), BF), dma((8,)), dma((8,)),
            pltpu.VMEM((256, 512), BF), pltpu.VMEM((256, 512), BF),
            pltpu.VMEM((256, 1024), BF), pltpu.VMEM((3, 64, 1024), BF), pltpu.VMEM((256, 1024), BF),
            dma((3,)), dma((3,)), dma((3,)), dma((3,)),
            pltpu.VMEM((256, 1024), BF),
            *[pltpu.VMEM((4, 4, 64, 512), BF)] * 3, *[pltpu.VMEM((4, 4, 128, 512), BF)] * 3,
            dma((3,)), dma((3,)),
        ],
        compiler_params=pltpu.CompilerParams(
            collective_id=1, has_side_effects=True, vmem_limit_bytes=VMEM_LIMIT
        ),
        cost_estimate=pl.CostEstimate(flops=7 * 10**9, bytes_accessed=24 * 2**20, transcendentals=2**18),
        name="decoder_scatter",
    )(*args)


def unpack_kernel(first, second, out_in, out, g_query, g_key, g_value, g_attn, g_in, g_out):
    out[...] = out_in[...]
    g_query[...] = first[pl.ds(0, 128)]
    g_attn[...] = first[pl.ds(128, 128)].T
    g_key[...] = second[pl.ds(0, 32)]
    g_value[...] = second[pl.ds(32, 32)]
    for n in range(2):
        cols = pl.ds(512 * n, 512)
        g_in[:, cols] = second[pl.ds(64 + 32 * n, 32)]
        g_out[:, cols] = second[pl.ds(128 + 32 * n, 32)]


def run_unpack(first, second, out):
    sds = jax.ShapeDtypeStruct
    return pl.pallas_call(
        unpack_kernel,
        out_shape=(
            sds((256, 1024), BF), sds((128, 512), F32), sds((32, 512), F32), sds((32, 512), F32),
            sds((512, 128), F32), sds((32, 1024), F32), sds((32, 1024), F32),
        ),
        in_specs=[VM] * 3,
        out_specs=(VM,) * 7,
        name="unpack",
    )(first, second, out)


def shards(
    enc_in, enc_gain, w_in, w_out, w_key, w_value, dec_in, w_query, w_attn_out, cotangent, group_doc, doc_lengths,
):
    normed, pre_act, activated, enc_out, kv, q_all, dm_all = run_encoder(
        enc_in[0], enc_gain[None, :], w_in, w_out, w_key, w_value, dec_in[0], w_query, w_attn_out, cotangent[0]
    )
    md, d_kv = run_attention(group_doc, doc_lengths, q_all, dm_all, kv)
    out, first, second = run_decoder(
        d_kv, md, dec_in[0], cotangent[0], w_attn_out, w_key, w_value, w_out, enc_out, normed, activated, pre_act
    )
    out, g_query, g_key, g_value, g_attn, g_in, g_out = run_unpack(first, second, out)
    return (out[None], g_query, g_key, g_value, g_attn, g_in, g_out.T)


def solution(mesh):
    placed = (
        P("grp", "seq", None),
        P(),
        P(None, "head"),
        P("head", None),
        P(None, "head"),
        P(None, "head"),
        P("grp", "seq", None),
        P(None, "head"),
        P("head", None),
        P("grp", "seq", None),
        P("grp", None),
        P("grp", None),
    )
    return jax.shard_map(
        shards,
        mesh=mesh,
        in_specs=placed,
        out_specs=(
            P("grp", "seq", "head"),
            P(("grp", "seq"), "head"),
            P(("grp", "seq"), "head"),
            P(("grp", "seq"), "head"),
            P("head", ("grp", "seq")),
            P(("grp", "seq"), "head"),
            P("head", ("grp", "seq")),
        ),
        check_vma=False,
    )
```

```python
import functools
import math

import jax
import jax.numpy as jnp
from jax import lax
from jax.experimental import pallas as pl
from jax.experimental.pallas import tpu as pltpu
from jax.sharding import PartitionSpec as P

HEAD_DIM = 128
GROUP = 256
N_SEQ = 16
N_HEAD = 4
EPSILON = 1e-06
MASKED = -1e30
SCALE = 1.0 / math.sqrt(HEAD_DIM)
SCALE2 = SCALE * math.log2(math.e)
MESH = pl.DeviceIdType.MESH
BF = jnp.bfloat16
F32 = jnp.float32
VMEM_LIMIT = 62 * 1024 * 1024
VM = pl.BlockSpec(memory_space=pltpu.VMEM)
ANY = pl.BlockSpec(memory_space=pl.ANY)


def mm(a, b):
    return lax.dot_general(a, b, (((1,), (0,)), ((), ())), preferred_element_type=F32)


def mm_rows(a, b):
    return lax.dot_general(a, b, (((0,), (0,)), ((), ())), preferred_element_type=F32)


def mm_cols(a, b):
    return lax.dot_general(a, b, (((1,), (1,)), ((), ())), preferred_element_type=F32)


def place():
    s = lax.axis_index("seq")
    return s >> 2, s & 3


def device_at(along, across):
    grp = lax.axis_index("grp")
    return (4 - 3 * grp) * along + (1 + 3 * grp) * across


def role():
    z, x = place()
    grp = lax.axis_index("grp")
    return (1 - grp) * z + grp * x, (1 - grp) * x + grp * z


def seq_copy(peer, src, dst, send_sem, recv_sem):
    return pltpu.make_async_remote_copy(
        src_ref=src,
        dst_ref=dst,
        send_sem=send_sem,
        recv_sem=recv_sem,
        device_id={"seq": peer},
        device_id_type=MESH,
    )


def x_copy(d, *rest):
    z, x = place()
    return seq_copy(4 * z + ((x + d) & 3), *rest)


def z_copy(d, *rest):
    z, x = place()
    return seq_copy(4 * ((z + d) & 3) + x, *rest)


def across_copy(d, *rest):
    along, across = role()
    return seq_copy(device_at(along, (across + d) & 3), *rest)


def along_copy(d, *rest):
    along, across = role()
    return seq_copy(device_at((along + d) & 3, across), *rest)


def greet(with_partner):
    z, x = place()
    h = lax.axis_index("head")
    barrier = pltpu.get_barrier_semaphore()
    for d in range(1, 4):
        for peer in (
            {"seq": 4 * z + ((x + d) & 3)},
            {"seq": 4 * ((z + d) & 3) + x},
            {"head": (h + d) & 3},
        ):
            pl.semaphore_signal(barrier, inc=1, device_id=peer, device_id_type=MESH)
    if with_partner:
        pl.semaphore_signal(
            barrier, inc=1, device_id={"grp": 1 - lax.axis_index("grp")}, device_id_type=MESH
        )


def met(with_partner):
    pl.semaphore_wait(pltpu.get_barrier_semaphore(), 10 if with_partner else 9)


def partner_copy(src, dst, send_sem, recv_sem):
    return pltpu.make_async_remote_copy(
        src_ref=src,
        dst_ref=dst,
        send_sem=send_sem,
        recv_sem=recv_sem,
        device_id={"grp": 1 - lax.axis_index("grp")},
        device_id_type=MESH,
    )


class Swap:
    def __init__(self, source, target, ss, rs):
        self.source, self.target, self.ss, self.rs = source, target, ss, rs
        self.x = role()[1]

    def sending(self, d):
        src = self.source.at[(self.x + d) & 3]
        return across_copy(d, src, self.target.at[self.x], self.ss.at[d - 1], self.rs.at[d - 1])

    def landing(self, d):
        ref = self.target.at[(self.x + 4 - d) & 3]
        return across_copy(d, ref, ref, self.ss.at[d - 1], self.rs.at[d - 1])

    def start(self):
        for d in (2, 1, 3):
            self.sending(d).start()

    def keep(self):
        self.target[self.x] = self.source[self.x]

    def finish(self):
        for d in (1, 3, 2):
            self.landing(d).wait_recv()

    def drain(self):
        for d in (1, 2, 3):
            self.sending(d).wait_send()


class Scatter:
    def __init__(self, blocks, n, slots, sums, last, ss, rs, ss2, rs2):
        self.blocks, self.n = blocks, n
        self.slots, self.sums, self.last = slots, sums, last
        self.ss, self.rs, self.ss2, self.rs2 = ss, rs, ss2, rs2
        self.z, self.x = place()

    def cut(self, half, d, chunk):
        rows = pl.ds(half * self.n, self.n)
        two = pl.ds(2 * chunk, 2)
        if half == 0:
            return self.blocks.at[two, (self.x + d) & 3, rows]
        return self.blocks.at[(self.z + d) & 3, two, rows]

    def first(self, half, d, chunk):
        move = x_copy if half == 0 else z_copy
        return move(
            d, self.cut(half, d, chunk), self.slots.at[half, d - 1, pl.ds(2 * chunk, 2)],
            self.ss.at[half, d - 1, chunk], self.rs.at[half, d - 1, chunk],
        )

    def second(self, half, d):
        move = z_copy if half == 0 else x_copy
        own = self.z if half == 0 else self.x
        return move(
            d, self.sums.at[half, (own + d) & 3], self.last.at[half, d - 1],
            self.ss2.at[half, d - 1], self.rs2.at[half, d - 1],
        )

    def start(self, half, chunk):
        for d in (2, 1, 3):
            self.first(half, d, chunk).start()

    def start_all(self):
        for chunk in (0, 1):
            for half in (0, 1):
                self.start(half, chunk)

    def middle(self, halves=(0, 1)):
        for half in halves:
            for chunk in (0, 1):
                for d in (1, 3, 2):
                    self.first(half, d, chunk).wait_recv()
                own = self.cut(half, 0, chunk)
                for k in range(2):
                    total = own[k].astype(F32)
                    for d in range(3):
                        total = total + self.slots[half, d, 2 * chunk + k].astype(F32)
                    self.sums[half, 2 * chunk + k] = total.astype(BF)
            for d in (2, 1, 3):
                self.second(half, d).start()

    def finish(self, half):
        for d in (1, 3, 2):
            self.second(half, d).wait_recv()
        own = self.z if half == 0 else self.x
        total = self.sums[half, own].astype(F32)
        for d in range(3):
            total = total + self.last[half, d].astype(F32)
        return total

    def drain(self):
        for half in (0, 1):
            for d in (1, 2, 3):
                for chunk in (0, 1):
                    self.first(half, d, chunk).wait_send()
                self.second(half, d).wait_send()

    @staticmethod
    def scratch(n, c):
        dma = pltpu.SemaphoreType.DMA
        return [
            pltpu.VMEM((2, 3, 4, n, c), BF), pltpu.VMEM((2, 4, n, c), BF), pltpu.VMEM((2, 3, n, c), BF),
            dma((2, 3, 2)), dma((2, 3, 2)), dma((2, 3)), dma((2, 3)),
        ]


def head_copy(d, src, dst, ss, rs):
    h = lax.axis_index("head")
    return pltpu.make_async_remote_copy(
        src_ref=src,
        dst_ref=dst,
        send_sem=ss.at[d - 1],
        recv_sem=rs.at[d - 1],
        device_id={"head": lax.rem(h + d, 4)},
        device_id_type=MESH,
    )


class HeadSum:
    def __init__(self, parts, slots, total, ss, rs, ss2, rs2):
        self.parts, self.slots, self.total = parts, slots, total
        self.ss, self.rs, self.ss2, self.rs2 = ss, rs, ss2, rs2
        self.h = lax.axis_index("head")

    def quarter(self, h):
        return pl.ds(pl.multiple_of(h * 64, 64), 64)

    def first(self, d):
        src = self.parts.at[self.quarter(lax.rem(self.h + d, 4))]
        return head_copy(d, src, self.slots.at[d - 1], self.ss, self.rs)

    def second(self, d):
        ref = self.total.at[self.quarter(self.h)]
        return head_copy(d, ref, ref, self.ss2, self.rs2)

    def second_landing(self, d):
        ref = self.total.at[self.quarter(lax.rem(self.h + 4 - d, 4))]
        return head_copy(d, ref, ref, self.ss2, self.rs2)

    def send(self):
        for d in (2, 1, 3):
            self.first(d).start()

    def receive(self):
        total = self.parts[self.quarter(self.h)].astype(F32)
        for d in (1, 3, 2):
            self.first(d).wait_recv()
            total = total + self.slots[d - 1].astype(F32)
        return total

    def share(self, total):
        self.total[self.quarter(self.h)] = total.astype(BF)
        for d in (2, 1, 3):
            self.second(d).start()

    def collect(self):
        for d in (1, 3, 2):
            self.second_landing(d).wait_recv()

    def drain(self):
        for d in (1, 2, 3):
            self.first(d).wait_send()
            self.second(d).wait_send()


def encoder_kernel(
    enc_in, gain, w_in, w_out, w_key, w_value, dec, w_query, w_attn, cot,
    normed_out, pre_out, act_out, enc_out_out, kv_out, q_out, dm_out,
    normed, pre_act, activated, enc_out, kv, q_all, dm_all, store_sem, kv_sem,
    v_in, v_out, v_key, v_value, v_dec, v_query, v_attn, v_cot, load_sem,
    parts, slots, hs1, hr1, hs2, hr2,
    q_send, dm_send, kv_send, qs, qr, ds, dr, ks, kr, zs, zr,
):
    pairs = (
        (w_in, v_in), (w_out, v_out), (dec, v_dec), (w_query, v_query),
        (w_key, v_key), (w_value, v_value), (cot, v_cot), (w_attn, v_attn),
    )
    loads = {id(v): pltpu.make_async_copy(a, v, load_sem.at[i]) for i, (a, v) in enumerate(pairs)}
    stores = [
        pltpu.make_async_copy(v, a, store_sem.at[i])
        for i, (v, a) in enumerate((
            (normed, normed_out), (pre_act, pre_out), (activated, act_out), (enc_out, enc_out_out),
            (q_all, q_out), (dm_all, dm_out),
        ))
    ]
    greet(False)
    for copy in loads.values():
        copy.start()
    along, across_at = role()
    encoded = enc_in[...].astype(F32)
    square = jnp.mean(encoded * encoded, axis=1, keepdims=True)
    normed[...] = (encoded * lax.rsqrt(square + EPSILON) * gain[...]).astype(BF)
    loads[id(v_in)].wait()
    for n in range(4):
        cols = pl.ds(n * 256, 256)
        pre = mm(normed[...], v_in[:, cols])
        pre_act[:, cols] = pre
        activated[:, cols] = (pre / (1.0 + jnp.exp(-pre))).astype(BF)
    loads[id(v_out)].wait()
    for n in range(4):
        cols = pl.ds(n * 256, 256)
        parts[:, cols] = mm(activated[...], v_out[:, cols]).astype(BF)
    met(False)
    for store in stores[:3]:
        store.start()
    across = HeadSum(parts, slots, enc_out, hs1, hr1, hs2, hr2)
    across.send()
    q_swap = Swap(q_send, q_all, qs, qr)
    dm_swap = Swap(dm_send, dm_all, ds, dr)
    kv_swap = Swap(kv_send, kv.at[pl.ds(4 * along, 4)], ks, kr)
    loads[id(v_dec)].wait()
    loads[id(v_query)].wait()
    for n in range(2):
        rows = mm(v_dec[...], v_query[:, pl.ds(n * 256, 256)]).astype(BF)
        q_send[2 * n], q_send[2 * n + 1] = rows[:, :128], rows[:, 128:]
    q_swap.start()
    own_rows = across.quarter(across.h)
    across.share(across.receive() + enc_in[own_rows].astype(F32))
    loads[id(v_cot)].wait()
    loads[id(v_attn)].wait()
    for n in range(2):
        rows = mm_cols(v_cot[...], v_attn[pl.ds(n * 256, 256), :]).astype(BF)
        dm_send[2 * n], dm_send[2 * n + 1] = rows[:, :128], rows[:, 128:]
    loads[id(v_key)].wait()
    loads[id(v_value)].wait()
    across.collect()
    for n in range(2):
        for weight, first in ((v_key, 0), (v_value, 128)):
            rows = mm(enc_out[...], weight[:, pl.ds(n * 256, 256)]).astype(BF)
            kv_send[2 * n, :, pl.ds(first, 128)] = rows[:, :128]
            kv_send[2 * n + 1, :, pl.ds(first, 128)] = rows[:, 128:]
    kv_swap.start()
    kv_swap.keep()

    def kv_part(k, back):
        return kv.at[4 * ((along + 4 - back) & 3) + ((across_at + k) & 3)]

    def move(k, d, back, slot):
        ref = kv_part(k, back)
        return along_copy(d, ref, ref, zs.at[slot, k], zr.at[slot, k])

    def keep(k, back):
        at = 4 * ((along + 4 - back) & 3) + ((across_at + k) & 3)
        return pltpu.make_async_copy(kv.at[at], kv_out.at[at], kv_sem.at[back, k])

    def ahead(k):
        return 1 if k % 2 == 0 else 3

    order = (0, 3, 1, 2)
    for d in (1, 3):
        move(0, d, 0, d - 1).start()
    for k in order[1:]:
        kv_swap.landing(4 - k).wait_recv()
        for d in (ahead(k), 4 - ahead(k)):
            move(k, d, 0, d - 1).start()
    dm_swap.start()
    for k in order:
        keep(k, 0).start()
        d = ahead(k)
        move(k, d, d, d - 1).wait_recv()
        move(k, d, d, 1).start()
        keep(k, d).start()
    across_at_rest = (q_swap, dm_swap)
    stores[3].start()
    for swap, store in zip(across_at_rest, stores[4:]):
        swap.keep()
        swap.finish()
        store.start()
    for k in order:
        d = 4 - ahead(k)
        move(k, d, d, d - 1).wait_recv()
        keep(k, d).start()
    for k in order:
        move(k, ahead(k), 2, 1).wait_recv()
        keep(k, 2).start()
    for k in order:
        for d in (1, 3):
            move(k, d, 0, d - 1).wait_send()
        move(k, ahead(k), ahead(k), 1).wait_send()
    for swap in (q_swap, dm_swap, kv_swap):
        swap.drain()
    across.drain()
    for store in stores:
        store.wait()
    for k in order:
        for back in range(4):
            keep(k, back).wait()


def run_encoder(*args):
    sds = jax.ShapeDtypeStruct
    dma = pltpu.SemaphoreType.DMA
    return pl.pallas_call(
        encoder_kernel,
        out_shape=(
            sds((256, 1024), BF), sds((256, 1024), F32), sds((256, 1024), BF), sds((256, 1024), BF),
            sds((16, 256, 256), BF), sds((4, 256, 128), BF), sds((4, 256, 128), BF),
        ),
        in_specs=[VM, VM] + [ANY] * 8,
        out_specs=(ANY,) * 7,
        scratch_shapes=[
            pltpu.VMEM((256, 1024), BF), pltpu.VMEM((256, 1024), F32), pltpu.VMEM((256, 1024), BF),
            pltpu.VMEM((256, 1024), BF), pltpu.VMEM((16, 256, 256), BF), pltpu.VMEM((4, 256, 128), BF),
            pltpu.VMEM((4, 256, 128), BF), dma((6,)), dma((4, 4)),
            pltpu.VMEM((1024, 1024), BF), pltpu.VMEM((1024, 1024), BF),
            pltpu.VMEM((1024, 512), BF), pltpu.VMEM((1024, 512), BF),
            pltpu.VMEM((256, 4096), BF), pltpu.VMEM((4096, 512), BF),
            pltpu.VMEM((512, 4096), BF), pltpu.VMEM((256, 4096), BF), dma((8,)),
            pltpu.VMEM((256, 1024), BF), pltpu.VMEM((3, 64, 1024), BF),
            dma((3,)), dma((3,)), dma((3,)), dma((3,)),
            pltpu.VMEM((4, 256, 128), BF), pltpu.VMEM((4, 256, 128), BF), pltpu.VMEM((4, 256, 256), BF),
            dma((3,)), dma((3,)), dma((3,)), dma((3,)), dma((3,)), dma((3,)), dma((3, 4)), dma((3, 4)),
        ],
        compiler_params=pltpu.CompilerParams(
            collective_id=0, has_side_effects=True, vmem_limit_bytes=VMEM_LIMIT
        ),
        cost_estimate=pl.CostEstimate(flops=5 * 10**9, bytes_accessed=24 * 2**20, transcendentals=2**18),
        name="encoder_gather",
    )(*args)


def attention_kernel(group_doc, doc_lengths, q_all, dm_all, kv, md, d_kv, scores, acc, d_acc, ends, begins, limits):
    along = role()[0]
    total = 0
    for j in range(8):
        total = total + doc_lengths[0, j]
        ends[j] = total
    for g in range(N_SEQ):
        doc = group_doc[0, g]
        limits[g] = ends[doc]
        begins[g] = ends[doc] - doc_lengths[0, doc]
    bounds = []
    for b in range(4):
        origin = device_at(along, b) * 256
        lo, hi = 0, 0
        for g in range(N_SEQ):
            lo = lo + jnp.where(limits[g] <= origin, 1, 0)
            hi = hi + jnp.where(begins[g] <= origin + 255, 1, 0)
        bounds.append((origin, lo, hi))
    low, high = bounds[0][1], bounds[3][2]

    def at(g):
        return device_at(g >> 2, g & 3)

    def clear(g, c):
        inside = (g >= low) & (g < high)

        @pl.when(inside)
        def _():
            d_acc[g] = jnp.zeros((256, 256), F32)

        @pl.when(jnp.logical_not(inside))
        def _():
            d_kv[at(g)] = jnp.zeros((256, 256), BF)

        return c

    lax.fori_loop(0, N_SEQ, clear, 0)
    for b in range(4):
        origin, lo, hi = bounds[b]
        position = origin + lax.broadcasted_iota(jnp.int32, (256, 1), 0)

        def score(g, m):
            s = mm_cols(q_all[b], kv[at(g), :, pl.ds(0, 128)]) * SCALE2
            seen = (position >= begins[g]) & (position < limits[g])
            s = jnp.where(seen, s, MASKED)
            scores[g] = s
            return jnp.maximum(m, jnp.max(s, axis=1, keepdims=True))

        top = lax.fori_loop(lo, hi, score, jnp.full((256, 1), MASKED, F32))
        acc[...] = jnp.zeros((256, 128), F32)

        def weigh(g, total):
            p = jnp.exp2(scores[g] - top)
            scores[g] = p
            acc[...] += mm(p.astype(BF), kv[at(g), :, pl.ds(128, 128)])
            return total + jnp.sum(p, axis=1, keepdims=True)

        total = lax.fori_loop(lo, hi, weigh, jnp.zeros((256, 1), F32))
        inverse = 1.0 / total
        rows = acc[...] * inverse
        md[b, :, pl.ds(0, 128)] = rows.astype(BF)
        inner = jnp.sum(rows * dm_all[b].astype(F32), axis=1, keepdims=True)
        acc[...] = jnp.zeros((256, 128), F32)
        query_t, upstream_t = q_all[b].T, dm_all[b].T

        def back(g, c):
            p = scores[g] * inverse
            dw = mm_cols(dm_all[b], kv[at(g), :, pl.ds(128, 128)])
            ds = (p * (dw - inner) * SCALE).astype(BF)
            acc[...] += mm(ds, kv[at(g), :, pl.ds(0, 128)])
            d_acc[g, pl.ds(0, 128)] += mm(query_t, ds)
            d_acc[g, pl.ds(128, 128)] += mm(upstream_t, p.astype(BF))
            return c

        lax.fori_loop(lo, hi, back, 0)
        md[b, :, pl.ds(128, 128)] = acc[...].astype(BF)

    def settle(g, c):
        d_kv[at(g)] = d_acc[g].astype(BF)
        return c

    lax.fori_loop(low, high, settle, 0)


def run_attention(*args):
    sds = jax.ShapeDtypeStruct
    smem = pl.BlockSpec(memory_space=pltpu.SMEM)
    return pl.pallas_call(
        attention_kernel,
        out_shape=(sds((4, 256, 256), BF), sds((16, 256, 256), BF)),
        in_specs=[smem, smem, VM, VM, VM],
        out_specs=(VM,) * 2,
        scratch_shapes=[
            pltpu.VMEM((16, 256, 256), F32), pltpu.VMEM((256, 128), F32), pltpu.VMEM((16, 256, 256), F32),
            pltpu.SMEM((8,), jnp.int32), pltpu.SMEM((16,), jnp.int32), pltpu.SMEM((16,), jnp.int32),
        ],
        compiler_params=pltpu.CompilerParams(vmem_limit_bytes=VMEM_LIMIT),
        cost_estimate=pl.CostEstimate(flops=2 * 10**9, bytes_accessed=6 * 2**20, transcendentals=2**20),
        name="attention",
    )(*args)


def decoder_kernel(
    d_kv, md, dec, cot, w_attn, w_key, w_value, w_out, enc_out, normed, activated, pre_act,
    out, first, second,
    *scratch,
):
    ring_a, ring_b, ring_c, ring_d = scratch[0:7], scratch[7:14], scratch[14:21], scratch[21:28]
    scratch = scratch[7:]
    v_dec, v_cot, v_attn, v_key, v_value, v_out, v_enc, v_normed, v_act, v_pre, load_sem = scratch[21:32]
    (
        m_all, ms, mr, row_slots, passing, zs, zr, row, kvg, ks, kr, mixed, mixed_t, query_t,
        out_own, out_send, out_recv, os, orr, stage, arrived, ps, pr,
    ) = scratch[32:55]
    (
        k_grad, v_grad, parts, slots, d_enc, hs1, hr1, hs2, hr2, d_pre,
        own_b, stage_b, arrived_b, own_c1, stage_c1, arrived_c1, own_c2, stage_c2, arrived_c2, cs, cr, enc_t, normed_t, d_enc_t,
    ) = scratch[55:]
    own_c, stage_c, arrived_c = (own_c1, own_c2), (stage_c1, stage_c2), (arrived_c1, arrived_c2)
    greet(True)
    loads = [
        pltpu.make_async_copy(a, v, load_sem.at[i])
        for i, (a, v) in enumerate((
            (w_attn, v_attn), (dec, v_dec), (cot, v_cot), (w_key, v_key), (w_value, v_value),
            (enc_out, v_enc), (w_out, v_out), (pre_act, v_pre), (activated, v_act), (normed, v_normed),
        ))
    ]
    for load in loads:
        load.start()
    met(True)
    along, across_at = role()
    h = lax.axis_index("head")
    grp = lax.axis_index("grp")
    m_swap = Swap(md, m_all, ms, mr)
    kv_swap = Swap(row, kvg, ks, kr)

    def mine(k, d):
        return d_kv.at[4 * ((along + d) & 3) + ((across_at + k) & 3)]

    def ahead(k):
        return 1 if k % 2 == 0 else 3

    def handed(k):
        return along_copy(ahead(k), mine(k, 2), passing.at[k], zs.at[1, k], zr.at[1, k])

    def term(k, d):
        src = passing.at[k] if d == ahead(k) else mine(k, d)
        return along_copy(d, src, row_slots.at[(d - 1) // 2, k], zs.at[d - 1, k], zr.at[d - 1, k])

    order = (2, 1, 3, 0)
    m_swap.start()
    for k in order:
        handed(k).start()
    for k in order:
        term(k, 4 - ahead(k)).start()
    m_swap.keep()
    loads[5].wait()
    enc_t[...] = v_enc[...].T
    m_swap.finish()
    for j in range(4):
        mixed[:, pl.ds(128 * j, 128)] = m_all[j, :, pl.ds(0, 128)]
        mixed_t[pl.ds(128 * j, 128), :] = m_all[j, :, pl.ds(0, 128)].T
        query_t[pl.ds(128 * j, 128), :] = m_all[j, :, pl.ds(128, 128)].T
    for k in order:
        handed(k).wait_recv()
        handed(k).wait_send()
        passing[k] = (passing[k].astype(F32) + mine(k, ahead(k))[...].astype(F32)).astype(BF)
        term(k, ahead(k)).start()

    def out_copy(d):
        return head_copy(d, out_send.at[d - 1], out_recv.at[d - 1], os, orr)

    def part(n, start):
        return pl.ds(pl.multiple_of(start + n * 256, 256), 256)

    loads[0].wait()
    for d in (2, 1, 3):
        start = ((h + d) & 3) * 1024
        for n in range(4):
            out_send[d - 1, :, pl.ds(n * 256, 256)] = mm(mixed[...], v_attn[:, part(n, start)]).astype(BF)
        if d != 2:
            out_copy(d).start()
    loads[1].wait()
    loads[2].wait()

    def products(u):
        t = (u + 8 * (1 - grp)) & 15
        here = pl.ds(pl.multiple_of(t * 256, 256), 256)
        return mm(query_t[...], v_dec[:, here]), mm(mixed_t[...], v_cot[:, here])

    def exchange(u):
        place_u = (u >> 1, pl.ds(2 * (u & 1), 2))
        return partner_copy(stage.at[place_u], arrived.at[place_u], ps.at[u], pr.at[u])

    def far(u, c):
        for which, value in enumerate(products(u)):
            for k in range(2):
                block = 2 * (u & 1) + k
                stage[u >> 1, block, :, pl.ds(128 * which, 128)] = value[:, 128 * k : 128 * (k + 1)].astype(BF)
        exchange(u).start()
        return c

    lax.fori_loop(0, 8, far, 0)
    for k in order:
        there = (across_at + k) & 3
        total = d_kv[4 * along + there].astype(F32)
        for d in (4 - ahead(k), ahead(k)):
            term(k, d).wait_recv()
            total = total + row_slots[(d - 1) // 2, k].astype(F32)
        row[there] = total.astype(BF)
        if k:
            kv_swap.sending(k).start()
    kv_swap.keep()

    def near(u, c):
        values = products(u + 8)
        exchange(u).wait_recv()
        for which, value in enumerate(values):
            for k in range(2):
                cols = pl.ds(128 * which, 128)
                block = 2 * (u & 1) + k
                both = value[:, 128 * k : 128 * (k + 1)].astype(BF) + arrived[u >> 1, block, :, cols]
                arrived[u >> 1, block, :, cols] = both
        return c

    scatter_a = Scatter(arrived, 256, *ring_a)
    lax.fori_loop(0, 4, near, 0)
    scatter_a.start(0, 0)
    lax.fori_loop(4, 8, near, 0)
    scatter_a.start(1, 0)
    scatter_a.start(0, 1)
    scatter_a.start(1, 1)
    kv_swap.finish()
    for j in range(4):
        k_grad[:, pl.ds(128 * j, 128)] = kvg[j, pl.ds(0, 128)].T
        v_grad[:, pl.ds(128 * j, 128)] = kvg[j, pl.ds(128, 128)].T
    loads[3].wait()
    loads[4].wait()
    for n in range(4):
        rows = pl.ds(n * 256, 256)
        value = mm_cols(k_grad[...], v_key[rows, :]) + mm_cols(v_grad[...], v_value[rows, :])
        parts[:, rows] = value.astype(BF)
    total_d = HeadSum(parts, slots, d_enc, hs1, hr1, hs2, hr2)
    total_d.send()

    for n in range(4):
        here = part(n, h * 1024)
        out_own[:, pl.ds(n * 256, 256)] = mm(mixed[...], v_attn[:, here]) + v_dec[:, here].astype(F32)
    far_from, near_from = (1 - grp) * 512, grp * 512

    def put(left_t, right, row_at, base, target):
        for n in range(2):
            value = mm(left_t[part(n, base), :], right[...])
            for k in range(8):
                block = n * 8 + k
                for m in range(value.shape[1] // 512):
                    piece = value[32 * k : 32 * (k + 1), 512 * m : 512 * (m + 1)].astype(BF)
                    target[block // 4, block % 4, pl.ds(row_at + 32 * m, 32)] = piece

    def add(own, more):
        def body(b, c):
            own[b] = own[b] + more[b]
            return c

        lax.fori_loop(0, 4, body, 0)

    swap_b = partner_copy(stage_b, arrived_b, cs.at[0], cr.at[0])
    put(enc_t, k_grad, 0, far_from, stage_b)
    put(enc_t, v_grad, 32, far_from, stage_b)
    swap_b.start()
    put(enc_t, k_grad, 0, near_from, own_b)
    put(enc_t, v_grad, 32, near_from, own_b)
    total_d.share(total_d.receive())
    swap_b.wait_recv()
    add(own_b, arrived_b)
    scatter_b = Scatter(own_b, 32, *ring_b)
    scatter_b.start_all()
    for load in loads[6:]:
        load.wait()
    normed_t[...] = v_normed[...].T
    total_d.collect()
    out_copy(2).start()
    d_enc_t[...] = d_enc[...].T
    swap_c = [partner_copy(stage_c[i], arrived_c[i], cs.at[1 + i], cr.at[1 + i]) for i in range(2)]
    put(d_enc_t, v_act, 0, far_from, stage_c[1])
    swap_c[1].start()
    for n in range(4):
        cols = pl.ds(n * 256, 256)
        pre = v_pre[:, cols]
        sig = 1.0 / (1.0 + jnp.exp(-pre))
        slope = sig * (1.0 + pre * (1.0 - sig))
        d_pre[:, cols] = (mm_cols(d_enc[...], v_out[cols, :]) * slope).astype(BF)
    put(normed_t, d_pre, 0, far_from, stage_c[0])
    swap_c[0].start()
    scatters_c = [Scatter(own_c[i], 32, *rings) for i, rings in enumerate((ring_c, ring_d))]
    put(d_enc_t, v_act, 0, near_from, own_c[1])
    swap_c[1].wait_recv()
    add(own_c[1], arrived_c[1])
    scatters_c[1].start_all()
    put(normed_t, d_pre, 0, near_from, own_c[0])
    swap_c[0].wait_recv()
    add(own_c[0], arrived_c[0])
    scatters_c[0].start_all()
    scatter_a.middle()
    scatter_b.middle()
    for half in range(2):
        first[pl.ds(256 * half, 256)] = scatter_a.finish(half)
    for half in range(2):
        second[pl.ds(32 * half, 32)] = scatter_b.finish(half)
    scatters_c[1].middle()
    scatters_c[0].middle()
    total = out_own[...]
    for d in (1, 3, 2):
        out_copy(d).wait_recv()
        total = total + out_recv[d - 1].astype(F32)
    out[...] = total.astype(BF)
    m_swap.drain()
    kv_swap.drain()
    for k in range(4):
        for d in (1, 3):
            term(k, d).wait_send()
    for d in (1, 2, 3):
        out_copy(d).wait_send()

    def sent(u, c):
        exchange(u).wait_send()
        return c

    lax.fori_loop(0, 8, sent, 0)
    scatter_a.drain()
    scatter_b.drain()
    total_d.drain()
    for copy in (swap_b, *swap_c):
        copy.wait_send()
    for i in (1, 0):
        for half in range(2):
            second[pl.ds(64 + 64 * i + 32 * half, 32)] = scatters_c[i].finish(half)
    for scatter in scatters_c:
        scatter.drain()


def run_decoder(*args):
    sds = jax.ShapeDtypeStruct
    dma = pltpu.SemaphoreType.DMA
    return pl.pallas_call(
        decoder_kernel,
        out_shape=(sds((256, 1024), BF), sds((512, 256), F32), sds((192, 512), F32)),
        in_specs=[VM, VM] + [ANY] * 10,
        out_specs=(VM,) * 3,
        scratch_shapes=[
            *Scatter.scratch(256, 256), *Scatter.scratch(32, 512), *Scatter.scratch(32, 512), *Scatter.scratch(32, 512),
            pltpu.VMEM((256, 4096), BF), pltpu.VMEM((256, 4096), BF), pltpu.VMEM((512, 4096), BF),
            pltpu.VMEM((1024, 512), BF), pltpu.VMEM((1024, 512), BF), pltpu.VMEM((1024, 1024), BF),
            pltpu.VMEM((256, 1024), BF), pltpu.VMEM((256, 1024), BF), pltpu.VMEM((256, 1024), BF),
            pltpu.VMEM((256, 1024), F32), dma((10,)),
            pltpu.VMEM((4, 256, 256), BF), dma((3,)), dma((3,)),
            pltpu.VMEM((2, 4, 256, 256), BF), pltpu.VMEM((4, 256, 256), BF), dma((3, 4)), dma((3, 4)),
            pltpu.VMEM((4, 256, 256), BF), pltpu.VMEM((4, 256, 256), BF), dma((3,)), dma((3,)),
            pltpu.VMEM((256, 512), BF), pltpu.VMEM((512, 256), BF), pltpu.VMEM((512, 256), BF),
            pltpu.VMEM((256, 1024), F32), pltpu.VMEM((3, 256, 1024), BF), pltpu.VMEM((3, 256, 1024), BF),
            dma((3,)), dma((3,)),
            pltpu.VMEM((4, 4, 512, 256), BF), pltpu.VMEM((4, 4, 512, 256), BF), dma((8,)), dma((8,)),
            pltpu.VMEM((256, 512), BF), pltpu.VMEM((256, 512), BF),
            pltpu.VMEM((256, 1024), BF), pltpu.VMEM((3, 64, 1024), BF), pltpu.VMEM((256, 1024), BF),
            dma((3,)), dma((3,)), dma((3,)), dma((3,)),
            pltpu.VMEM((256, 1024), BF),
            *[pltpu.VMEM((4, 4, 64, 512), BF)] * 9,
            dma((3,)), dma((3,)),
            *[pltpu.VMEM((1024, 256), BF)] * 3,
        ],
        compiler_params=pltpu.CompilerParams(
            collective_id=1, has_side_effects=True, vmem_limit_bytes=VMEM_LIMIT
        ),
        cost_estimate=pl.CostEstimate(flops=7 * 10**9, bytes_accessed=24 * 2**20, transcendentals=2**18),
        name="decoder_scatter",
    )(*args)


def unpack_kernel(first, second, out_in, out, g_query, g_key, g_value, g_attn, g_in, g_out):
    out[...] = out_in[...]
    g_query[...] = first[:, pl.ds(0, 128)].T
    g_attn[...] = first[:, pl.ds(128, 128)]
    g_key[...] = second[pl.ds(0, 32)]
    g_value[...] = second[pl.ds(32, 32)]
    for n in range(2):
        cols = pl.ds(512 * n, 512)
        g_in[:, cols] = second[pl.ds(64 + 32 * n, 32)]
        g_out[:, cols] = second[pl.ds(128 + 32 * n, 32)]


def run_unpack(first, second, out):
    sds = jax.ShapeDtypeStruct
    return pl.pallas_call(
        unpack_kernel,
        out_shape=(
            sds((256, 1024), BF), sds((128, 512), F32), sds((32, 512), F32), sds((32, 512), F32),
            sds((512, 128), F32), sds((32, 1024), F32), sds((32, 1024), F32),
        ),
        in_specs=[VM] * 3,
        out_specs=(VM,) * 7,
        name="unpack",
    )(first, second, out)


def shards(
    enc_in, enc_gain, w_in, w_out, w_key, w_value, dec_in, w_query, w_attn_out, cotangent, group_doc, doc_lengths,
):
    normed, pre_act, activated, enc_out, kv, q_all, dm_all = run_encoder(
        enc_in[0], enc_gain[None, :], w_in, w_out, w_key, w_value, dec_in[0], w_query, w_attn_out, cotangent[0]
    )
    md, d_kv = run_attention(group_doc, doc_lengths, q_all, dm_all, kv)
    out, first, second = run_decoder(
        d_kv, md, dec_in[0], cotangent[0], w_attn_out, w_key, w_value, w_out, enc_out, normed, activated, pre_act
    )
    out, g_query, g_key, g_value, g_attn, g_in, g_out = run_unpack(first, second, out)
    return (out[None], g_query, g_key, g_value, g_attn, g_in, g_out.T)


def solution(mesh):
    placed = (
        P("grp", "seq", None),
        P(),
        P(None, "head"),
        P("head", None),
        P(None, "head"),
        P(None, "head"),
        P("grp", "seq", None),
        P(None, "head"),
        P("head", None),
        P("grp", "seq", None),
        P("grp", None),
        P("grp", None),
    )
    return jax.shard_map(
        shards,
        mesh=mesh,
        in_specs=placed,
        out_specs=(
            P("grp", "seq", "head"),
            P(("grp", "seq"), "head"),
            P(("grp", "seq"), "head"),
            P(("grp", "seq"), "head"),
            P("head", ("grp", "seq")),
            P(("grp", "seq"), "head"),
            P("head", ("grp", "seq")),
        ),
        check_vma=False,
    )
```

```python
import functools
import math

import jax
import jax.numpy as jnp
from jax import lax
from jax.experimental import pallas as pl
from jax.experimental.pallas import tpu as pltpu
from jax.sharding import PartitionSpec as P

HEAD_DIM = 128
GROUP = 256
N_SEQ = 16
N_HEAD = 4
EPSILON = 1e-06
MASKED = -1e30
SCALE = 1.0 / math.sqrt(HEAD_DIM)
SCALE2 = SCALE * math.log2(math.e)
MESH = pl.DeviceIdType.MESH
BF = jnp.bfloat16
F32 = jnp.float32
VMEM_LIMIT = 62 * 1024 * 1024
VM = pl.BlockSpec(memory_space=pltpu.VMEM)
ANY = pl.BlockSpec(memory_space=pl.ANY)


def mm(a, b):
    return lax.dot_general(a, b, (((1,), (0,)), ((), ())), preferred_element_type=F32)


def mm_rows(a, b):
    return lax.dot_general(a, b, (((0,), (0,)), ((), ())), preferred_element_type=F32)


def mm_cols(a, b):
    return lax.dot_general(a, b, (((1,), (1,)), ((), ())), preferred_element_type=F32)


def place():
    s = lax.axis_index("seq")
    return s >> 2, s & 3


def device_at(along, across):
    grp = lax.axis_index("grp")
    return (4 - 3 * grp) * along + (1 + 3 * grp) * across


def role():
    z, x = place()
    grp = lax.axis_index("grp")
    return (1 - grp) * z + grp * x, (1 - grp) * x + grp * z


def seq_copy(peer, src, dst, send_sem, recv_sem):
    return pltpu.make_async_remote_copy(
        src_ref=src,
        dst_ref=dst,
        send_sem=send_sem,
        recv_sem=recv_sem,
        device_id={"seq": peer},
        device_id_type=MESH,
    )


def x_copy(d, *rest):
    z, x = place()
    return seq_copy(4 * z + ((x + d) & 3), *rest)


def z_copy(d, *rest):
    z, x = place()
    return seq_copy(4 * ((z + d) & 3) + x, *rest)


def across_copy(d, *rest):
    along, across = role()
    return seq_copy(device_at(along, (across + d) & 3), *rest)


def along_copy(d, *rest):
    along, across = role()
    return seq_copy(device_at((along + d) & 3, across), *rest)


def greet(with_partner):
    z, x = place()
    h = lax.axis_index("head")
    barrier = pltpu.get_barrier_semaphore()
    for d in range(1, 4):
        for peer in (
            {"seq": 4 * z + ((x + d) & 3)},
            {"seq": 4 * ((z + d) & 3) + x},
            {"head": (h + d) & 3},
        ):
            pl.semaphore_signal(barrier, inc=1, device_id=peer, device_id_type=MESH)
    if with_partner:
        pl.semaphore_signal(
            barrier, inc=1, device_id={"grp": 1 - lax.axis_index("grp")}, device_id_type=MESH
        )


def met(with_partner):
    pl.semaphore_wait(pltpu.get_barrier_semaphore(), 10 if with_partner else 9)


def partner_copy(src, dst, send_sem, recv_sem):
    return pltpu.make_async_remote_copy(
        src_ref=src,
        dst_ref=dst,
        send_sem=send_sem,
        recv_sem=recv_sem,
        device_id={"grp": 1 - lax.axis_index("grp")},
        device_id_type=MESH,
    )


class Swap:
    def __init__(self, source, target, ss, rs):
        self.source, self.target, self.ss, self.rs = source, target, ss, rs
        self.x = role()[1]

    def sending(self, d):
        src = self.source.at[(self.x + d) & 3]
        return across_copy(d, src, self.target.at[self.x], self.ss.at[d - 1], self.rs.at[d - 1])

    def landing(self, d):
        ref = self.target.at[(self.x + 4 - d) & 3]
        return across_copy(d, ref, ref, self.ss.at[d - 1], self.rs.at[d - 1])

    def start(self):
        for d in (2, 1, 3):
            self.sending(d).start()

    def keep(self):
        self.target[self.x] = self.source[self.x]

    def finish(self):
        for d in (1, 3, 2):
            self.landing(d).wait_recv()

    def drain(self):
        for d in (1, 2, 3):
            self.sending(d).wait_send()


class Scatter:
    def __init__(self, blocks, n, slots, passing, sums, last, ss, rs, ss2, rs2):
        self.blocks, self.n = blocks, n
        self.slots, self.passing, self.sums, self.last = slots, passing, sums, last
        self.ss, self.rs, self.ss2, self.rs2 = ss, rs, ss2, rs2
        self.z, self.x = place()

    def cut(self, half, d, chunk):
        rows = pl.ds(half * self.n, self.n)
        two = pl.ds(2 * chunk, 2)
        if half == 0:
            return self.blocks.at[two, (self.x + d) & 3, rows]
        return self.blocks.at[(self.z + d) & 3, two, rows]

    def ahead(self, chunk):
        return 3 if chunk else 1

    def handed(self, half, chunk):
        move = x_copy if half == 0 else z_copy
        return move(
            self.ahead(chunk), self.cut(half, 2, chunk), self.passing.at[half, chunk],
            self.ss.at[half, 1, chunk], self.rs.at[half, 1, chunk],
        )

    def first(self, half, d, chunk):
        move = x_copy if half == 0 else z_copy
        src = self.passing.at[half, chunk] if d == self.ahead(chunk) else self.cut(half, d, chunk)
        return move(
            d, src, self.slots.at[half, (d - 1) // 2, pl.ds(2 * chunk, 2)],
            self.ss.at[half, d - 1, chunk], self.rs.at[half, d - 1, chunk],
        )

    def second(self, half, d):
        move = z_copy if half == 0 else x_copy
        own = self.z if half == 0 else self.x
        return move(
            d, self.sums.at[half, (own + d) & 3], self.last.at[half, d - 1],
            self.ss2.at[half, d - 1], self.rs2.at[half, d - 1],
        )

    def start(self, half, chunk):
        self.handed(half, chunk).start()
        self.first(half, 4 - self.ahead(chunk), chunk).start()

    def relay(self):
        for chunk in (0, 1):
            for half in (0, 1):
                self.handed(half, chunk).wait()
                own = self.cut(half, self.ahead(chunk), chunk)
                for k in range(2):
                    self.passing[half, chunk, k] = self.passing[half, chunk, k] + own[k]
                self.first(half, self.ahead(chunk), chunk).start()

    def start_all(self):
        for chunk in (0, 1):
            for half in (0, 1):
                self.start(half, chunk)

    def middle(self, halves=(0, 1)):
        for half in halves:
            for chunk in (0, 1):
                for d in (4 - self.ahead(chunk), self.ahead(chunk)):
                    self.first(half, d, chunk).wait_recv()
                own = self.cut(half, 0, chunk)
                for k in range(2):
                    total = own[k].astype(F32)
                    for d in range(2):
                        total = total + self.slots[half, d, 2 * chunk + k].astype(F32)
                    self.sums[half, 2 * chunk + k] = total.astype(BF)
            for d in (2, 1, 3):
                self.second(half, d).start()

    def finish(self, half):
        for d in (1, 3, 2):
            self.second(half, d).wait_recv()
        own = self.z if half == 0 else self.x
        total = self.sums[half, own].astype(F32)
        for d in range(3):
            total = total + self.last[half, d].astype(F32)
        return total

    def drain(self):
        for half in (0, 1):
            for chunk in (0, 1):
                for d in (1, 3):
                    self.first(half, d, chunk).wait_send()
            for d in (1, 2, 3):
                self.second(half, d).wait_send()

    @staticmethod
    def scratch(n, c):
        dma = pltpu.SemaphoreType.DMA
        return [
            pltpu.VMEM((2, 2, 4, n, c), BF), pltpu.VMEM((2, 2, 2, n, c), BF), pltpu.VMEM((2, 4, n, c), BF), pltpu.VMEM((2, 3, n, c), BF),
            dma((2, 3, 2)), dma((2, 3, 2)), dma((2, 3)), dma((2, 3)),
        ]


def head_copy(d, src, dst, ss, rs):
    h = lax.axis_index("head")
    return pltpu.make_async_remote_copy(
        src_ref=src,
        dst_ref=dst,
        send_sem=ss.at[d - 1],
        recv_sem=rs.at[d - 1],
        device_id={"head": lax.rem(h + d, 4)},
        device_id_type=MESH,
    )


class HeadSum:
    def __init__(self, parts, slots, total, ss, rs, ss2, rs2):
        self.parts, self.slots, self.total = parts, slots, total
        self.ss, self.rs, self.ss2, self.rs2 = ss, rs, ss2, rs2
        self.h = lax.axis_index("head")

    def quarter(self, h):
        return pl.ds(pl.multiple_of(h * 64, 64), 64)

    def first(self, d):
        src = self.parts.at[self.quarter(lax.rem(self.h + d, 4))]
        return head_copy(d, src, self.slots.at[d - 1], self.ss, self.rs)

    def second(self, d):
        ref = self.total.at[self.quarter(self.h)]
        return head_copy(d, ref, ref, self.ss2, self.rs2)

    def second_landing(self, d):
        ref = self.total.at[self.quarter(lax.rem(self.h + 4 - d, 4))]
        return head_copy(d, ref, ref, self.ss2, self.rs2)

    def send(self):
        for d in (2, 1, 3):
            self.first(d).start()

    def receive(self):
        total = self.parts[self.quarter(self.h)].astype(F32)
        for d in (1, 3, 2):
            self.first(d).wait_recv()
            total = total + self.slots[d - 1].astype(F32)
        return total

    def share(self, total):
        self.total[self.quarter(self.h)] = total.astype(BF)
        for d in (2, 1, 3):
            self.second(d).start()

    def collect(self):
        for d in (1, 3, 2):
            self.second_landing(d).wait_recv()

    def drain(self):
        for d in (1, 2, 3):
            self.first(d).wait_send()
            self.second(d).wait_send()


def encoder_kernel(
    enc_in, gain, w_in, w_out, w_key, w_value, dec, w_query, w_attn, cot,
    normed_out, pre_out, act_out, enc_out_out, kv_out, q_out, dm_out,
    normed, pre_act, activated, enc_out, kv, q_all, dm_all, store_sem, kv_sem,
    v_in, v_out, v_key, v_value, v_dec, v_query, v_attn, v_cot, load_sem,
    parts, slots, hs1, hr1, hs2, hr2,
    q_send, dm_send, kv_send, qs, qr, ds, dr, ks, kr, zs, zr,
):
    pairs = (
        (w_in, v_in), (w_out, v_out), (dec, v_dec), (w_query, v_query),
        (w_key, v_key), (w_value, v_value), (cot, v_cot), (w_attn, v_attn),
    )
    loads = {id(v): pltpu.make_async_copy(a, v, load_sem.at[i]) for i, (a, v) in enumerate(pairs)}
    stores = [
        pltpu.make_async_copy(v, a, store_sem.at[i])
        for i, (v, a) in enumerate((
            (normed, normed_out), (pre_act, pre_out), (activated, act_out), (enc_out, enc_out_out),
            (q_all, q_out), (dm_all, dm_out),
        ))
    ]
    greet(False)
    for copy in loads.values():
        copy.start()
    along, across_at = role()
    encoded = enc_in[...].astype(F32)
    square = jnp.mean(encoded * encoded, axis=1, keepdims=True)
    normed[...] = (encoded * lax.rsqrt(square + EPSILON) * gain[...]).astype(BF)
    loads[id(v_in)].wait()
    for n in range(4):
        cols = pl.ds(n * 256, 256)
        pre = mm(normed[...], v_in[:, cols])
        pre_act[:, cols] = pre
        activated[:, cols] = (pre / (1.0 + jnp.exp(-pre))).astype(BF)
    loads[id(v_out)].wait()
    for n in range(4):
        cols = pl.ds(n * 256, 256)
        parts[:, cols] = mm(activated[...], v_out[:, cols]).astype(BF)
    met(False)
    for store in stores[:3]:
        store.start()
    across = HeadSum(parts, slots, enc_out, hs1, hr1, hs2, hr2)
    across.send()
    q_swap = Swap(q_send, q_all, qs, qr)
    dm_swap = Swap(dm_send, dm_all, ds, dr)
    kv_swap = Swap(kv_send, kv.at[pl.ds(4 * along, 4)], ks, kr)
    loads[id(v_dec)].wait()
    loads[id(v_query)].wait()
    for n in range(2):
        rows = mm(v_dec[...], v_query[:, pl.ds(n * 256, 256)]).astype(BF)
        q_send[2 * n], q_send[2 * n + 1] = rows[:, :128], rows[:, 128:]
    q_swap.start()
    own_rows = across.quarter(across.h)
    across.share(across.receive() + enc_in[own_rows].astype(F32))
    loads[id(v_cot)].wait()
    loads[id(v_attn)].wait()
    for n in range(2):
        rows = mm_cols(v_cot[...], v_attn[pl.ds(n * 256, 256), :]).astype(BF)
        dm_send[2 * n], dm_send[2 * n + 1] = rows[:, :128], rows[:, 128:]
    loads[id(v_key)].wait()
    loads[id(v_value)].wait()
    across.collect()
    for n in range(2):
        for weight, first in ((v_key, 0), (v_value, 128)):
            rows = mm(enc_out[...], weight[:, pl.ds(n * 256, 256)]).astype(BF)
            kv_send[2 * n, :, pl.ds(first, 128)] = rows[:, :128]
            kv_send[2 * n + 1, :, pl.ds(first, 128)] = rows[:, 128:]
    kv_swap.start()
    kv_swap.keep()

    def kv_part(k, back):
        return kv.at[4 * ((along + 4 - back) & 3) + ((across_at + k) & 3)]

    def move(k, d, back, slot):
        ref = kv_part(k, back)
        return along_copy(d, ref, ref, zs.at[slot, k], zr.at[slot, k])

    def keep(k, back):
        at = 4 * ((along + 4 - back) & 3) + ((across_at + k) & 3)
        return pltpu.make_async_copy(kv.at[at], kv_out.at[at], kv_sem.at[back, k])

    def ahead(k):
        return 1 if k % 2 == 0 else 3

    order = (0, 3, 1, 2)
    for d in (1, 3):
        move(0, d, 0, d - 1).start()
    for k in order[1:]:
        kv_swap.landing(4 - k).wait_recv()
        for d in (ahead(k), 4 - ahead(k)):
            move(k, d, 0, d - 1).start()
    dm_swap.start()
    for k in order:
        keep(k, 0).start()
        d = ahead(k)
        move(k, d, d, d - 1).wait_recv()
        move(k, d, d, 1).start()
        keep(k, d).start()
    across_at_rest = (q_swap, dm_swap)
    stores[3].start()
    for swap, store in zip(across_at_rest, stores[4:]):
        swap.keep()
        swap.finish()
        store.start()
    for k in order:
        d = 4 - ahead(k)
        move(k, d, d, d - 1).wait_recv()
        keep(k, d).start()
    for k in order:
        move(k, ahead(k), 2, 1).wait_recv()
        keep(k, 2).start()
    for k in order:
        for d in (1, 3):
            move(k, d, 0, d - 1).wait_send()
        move(k, ahead(k), ahead(k), 1).wait_send()
    for swap in (q_swap, dm_swap, kv_swap):
        swap.drain()
    across.drain()
    for store in stores:
        store.wait()
    for k in order:
        for back in range(4):
            keep(k, back).wait()


def run_encoder(*args):
    sds = jax.ShapeDtypeStruct
    dma = pltpu.SemaphoreType.DMA
    return pl.pallas_call(
        encoder_kernel,
        out_shape=(
            sds((256, 1024), BF), sds((256, 1024), F32), sds((256, 1024), BF), sds((256, 1024), BF),
            sds((16, 256, 256), BF), sds((4, 256, 128), BF), sds((4, 256, 128), BF),
        ),
        in_specs=[VM, VM] + [ANY] * 8,
        out_specs=(ANY,) * 7,
        scratch_shapes=[
            pltpu.VMEM((256, 1024), BF), pltpu.VMEM((256, 1024), F32), pltpu.VMEM((256, 1024), BF),
            pltpu.VMEM((256, 1024), BF), pltpu.VMEM((16, 256, 256), BF), pltpu.VMEM((4, 256, 128), BF),
            pltpu.VMEM((4, 256, 128), BF), dma((6,)), dma((4, 4)),
            pltpu.VMEM((1024, 1024), BF), pltpu.VMEM((1024, 1024), BF),
            pltpu.VMEM((1024, 512), BF), pltpu.VMEM((1024, 512), BF),
            pltpu.VMEM((256, 4096), BF), pltpu.VMEM((4096, 512), BF),
            pltpu.VMEM((512, 4096), BF), pltpu.VMEM((256, 4096), BF), dma((8,)),
            pltpu.VMEM((256, 1024), BF), pltpu.VMEM((3, 64, 1024), BF),
            dma((3,)), dma((3,)), dma((3,)), dma((3,)),
            pltpu.VMEM((4, 256, 128), BF), pltpu.VMEM((4, 256, 128), BF), pltpu.VMEM((4, 256, 256), BF),
            dma((3,)), dma((3,)), dma((3,)), dma((3,)), dma((3,)), dma((3,)), dma((3, 4)), dma((3, 4)),
        ],
        compiler_params=pltpu.CompilerParams(
            collective_id=0, has_side_effects=True, vmem_limit_bytes=VMEM_LIMIT
        ),
        cost_estimate=pl.CostEstimate(flops=5 * 10**9, bytes_accessed=24 * 2**20, transcendentals=2**18),
        name="encoder_gather",
    )(*args)


def attention_kernel(group_doc, doc_lengths, q_all, dm_all, kv, md, d_kv, scores, acc, d_acc, ends, begins, limits):
    along = role()[0]
    total = 0
    for j in range(8):
        total = total + doc_lengths[0, j]
        ends[j] = total
    for g in range(N_SEQ):
        doc = group_doc[0, g]
        limits[g] = ends[doc]
        begins[g] = ends[doc] - doc_lengths[0, doc]
    bounds = []
    for b in range(4):
        origin = device_at(along, b) * 256
        lo, hi = 0, 0
        for g in range(N_SEQ):
            lo = lo + jnp.where(limits[g] <= origin, 1, 0)
            hi = hi + jnp.where(begins[g] <= origin + 255, 1, 0)
        bounds.append((origin, lo, hi))
    low, high = bounds[0][1], bounds[3][2]

    def at(g):
        return device_at(g >> 2, g & 3)

    def clear(g, c):
        inside = (g >= low) & (g < high)

        @pl.when(inside)
        def _():
            d_acc[g] = jnp.zeros((256, 256), F32)

        @pl.when(jnp.logical_not(inside))
        def _():
            d_kv[at(g)] = jnp.zeros((256, 256), BF)

        return c

    lax.fori_loop(0, N_SEQ, clear, 0)
    for b in range(4):
        origin, lo, hi = bounds[b]
        position = origin + lax.broadcasted_iota(jnp.int32, (256, 1), 0)

        steps = (hi - lo + 1) >> 1

        def pair(i):
            g = lo + 2 * i
            return g, jnp.minimum(g + 1, N_SEQ - 1), g + 1 < hi

        def score(g, valid):
            s = mm_cols(q_all[b], kv[at(g), :, pl.ds(0, 128)]) * SCALE2
            first = begins[g] if valid is None else jnp.where(valid, begins[g], 1 << 30)
            return jnp.where((position >= first) & (position < limits[g]), s, MASKED)

        acc[...] = jnp.zeros((256, 128), F32)

        def weigh(i, carry):
            top, total = carry
            g, other, valid = pair(i)
            s, r = score(g, None), score(other, valid)
            scores[2 * i], scores[2 * i + 1] = s, r
            peak = jnp.maximum(top, jnp.max(jnp.maximum(s, r), axis=1, keepdims=True))
            shrink = jnp.exp2(top - peak)
            p, o = jnp.exp2(s - peak), jnp.exp2(r - peak)
            more = mm(p.astype(BF), kv[at(g), :, pl.ds(128, 128)])
            more = more + mm(o.astype(BF), kv[at(other), :, pl.ds(128, 128)])
            acc[...] = acc[...] * shrink + more
            return peak, total * shrink + jnp.sum(p + o, axis=1, keepdims=True)

        start = (jnp.full((256, 1), MASKED, F32), jnp.zeros((256, 1), F32))
        top, total = lax.fori_loop(0, steps, weigh, start)
        rows = acc[...] / total
        level = top + jnp.log2(total)
        md[b, :, pl.ds(0, 128)] = rows.astype(BF)
        inner = jnp.sum(rows * dm_all[b].astype(F32), axis=1, keepdims=True)
        acc[...] = jnp.zeros((256, 128), F32)
        query_t, upstream_t = q_all[b].T, dm_all[b].T

        def back(i, c):
            g, other, _ = pair(i)
            more = acc[...]
            terms = []
            for n, at_g in ((0, g), (1, other)):
                p = jnp.exp2(scores[2 * i + n] - level)
                dw = mm_cols(dm_all[b], kv[at(at_g), :, pl.ds(128, 128)])
                ds = (p * (dw - inner) * SCALE).astype(BF)
                more = more + mm(ds, kv[at(at_g), :, pl.ds(0, 128)])
                terms.append((at_g, mm(query_t, ds), mm(upstream_t, p.astype(BF))))
            acc[...] = more
            for at_g, d_key, d_value in terms:
                d_acc[at_g, pl.ds(0, 128)] += d_key
                d_acc[at_g, pl.ds(128, 128)] += d_value
            return c

        lax.fori_loop(0, steps, back, 0)
        md[b, :, pl.ds(128, 128)] = acc[...].astype(BF)

    def settle(g, c):
        d_kv[at(g)] = d_acc[g].astype(BF)
        return c

    lax.fori_loop(low, high, settle, 0)


def run_attention(*args):
    sds = jax.ShapeDtypeStruct
    smem = pl.BlockSpec(memory_space=pltpu.SMEM)
    return pl.pallas_call(
        attention_kernel,
        out_shape=(sds((4, 256, 256), BF), sds((16, 256, 256), BF)),
        in_specs=[smem, smem, VM, VM, VM],
        out_specs=(VM,) * 2,
        scratch_shapes=[
            pltpu.VMEM((16, 256, 256), F32), pltpu.VMEM((256, 128), F32), pltpu.VMEM((16, 256, 256), F32),
            pltpu.SMEM((8,), jnp.int32), pltpu.SMEM((16,), jnp.int32), pltpu.SMEM((16,), jnp.int32),
        ],
        compiler_params=pltpu.CompilerParams(vmem_limit_bytes=VMEM_LIMIT),
        cost_estimate=pl.CostEstimate(flops=2 * 10**9, bytes_accessed=6 * 2**20, transcendentals=2**20),
        name="attention",
    )(*args)


def decoder_kernel(
    d_kv, md, dec, cot, w_attn, w_key, w_value, w_out, enc_out, normed, activated, pre_act,
    out, first, second,
    *scratch,
):
    ring_a, ring_b, ring_c, ring_d = (scratch[8 * i : 8 * i + 8] for i in range(4))
    scratch = scratch[11:]
    v_dec, v_cot, v_attn, v_key, v_value, v_out, v_enc, v_normed, v_act, v_pre, load_sem = scratch[21:32]
    (
        m_all, ms, mr, row_slots, passing, zs, zr, row, kvg, ks, kr, mixed, mixed_t, query_t,
        out_own, out_send, out_recv, os, orr, stage, arrived, ps, pr,
    ) = scratch[32:55]
    (
        k_grad, v_grad, parts, slots, d_enc, hs1, hr1, hs2, hr2, d_pre,
        own_b, stage_b, arrived_b, own_c1, stage_c1, arrived_c1, own_c2, stage_c2, arrived_c2, cs, cr, enc_t, normed_t, d_enc_t,
    ) = scratch[55:]
    own_c, stage_c, arrived_c = (own_c1, own_c2), (stage_c1, stage_c2), (arrived_c1, arrived_c2)
    greet(True)
    loads = [
        pltpu.make_async_copy(a, v, load_sem.at[i])
        for i, (a, v) in enumerate((
            (w_attn, v_attn), (dec, v_dec), (cot, v_cot), (w_key, v_key), (w_value, v_value),
            (enc_out, v_enc), (w_out, v_out), (pre_act, v_pre), (activated, v_act), (normed, v_normed),
        ))
    ]
    for load in loads:
        load.start()
    met(True)
    along, across_at = role()
    h = lax.axis_index("head")
    grp = lax.axis_index("grp")
    m_swap = Swap(md, m_all, ms, mr)
    kv_swap = Swap(row, kvg, ks, kr)

    def mine(k, d):
        return d_kv.at[4 * ((along + d) & 3) + ((across_at + k) & 3)]

    def ahead(k):
        return 1 if k % 2 == 0 else 3

    def handed(k):
        return along_copy(ahead(k), mine(k, 2), passing.at[k], zs.at[1, k], zr.at[1, k])

    def term(k, d):
        src = passing.at[k] if d == ahead(k) else mine(k, d)
        return along_copy(d, src, row_slots.at[(d - 1) // 2, k], zs.at[d - 1, k], zr.at[d - 1, k])

    order = (2, 1, 3, 0)
    m_swap.start()
    for k in order:
        handed(k).start()
    for k in order:
        term(k, 4 - ahead(k)).start()
    m_swap.keep()
    loads[5].wait()
    enc_t[...] = v_enc[...].T
    m_swap.finish()
    for j in range(4):
        mixed[:, pl.ds(128 * j, 128)] = m_all[j, :, pl.ds(0, 128)]
        mixed_t[pl.ds(128 * j, 128), :] = m_all[j, :, pl.ds(0, 128)].T
        query_t[pl.ds(128 * j, 128), :] = m_all[j, :, pl.ds(128, 128)].T
    for k in order:
        handed(k).wait_recv()
        handed(k).wait_send()
        passing[k] = (passing[k].astype(F32) + mine(k, ahead(k))[...].astype(F32)).astype(BF)
        term(k, ahead(k)).start()

    def out_copy(d):
        return head_copy(d, out_send.at[d - 1], out_recv.at[d - 1], os, orr)

    def part(n, start):
        return pl.ds(pl.multiple_of(start + n * 256, 256), 256)

    loads[1].wait()
    loads[2].wait()

    def products(u):
        t = (u + 8 * (1 - grp)) & 15
        here = pl.ds(pl.multiple_of(t * 256, 256), 256)
        return mm(query_t[...], v_dec[:, here]), mm(mixed_t[...], v_cot[:, here])

    def exchange(u):
        place_u = (u >> 1, pl.ds(2 * (u & 1), 2))
        return partner_copy(stage.at[place_u], arrived.at[place_u], ps.at[u], pr.at[u])

    def far(u, c):
        for which, value in enumerate(products(u)):
            for k in range(2):
                block = 2 * (u & 1) + k
                stage[u >> 1, block, :, pl.ds(128 * which, 128)] = value[:, 128 * k : 128 * (k + 1)].astype(BF)
        exchange(u).start()
        return c

    lax.fori_loop(0, 8, far, 0)
    for k in order:
        there = (across_at + k) & 3
        total = d_kv[4 * along + there].astype(F32)
        for d in (4 - ahead(k), ahead(k)):
            term(k, d).wait_recv()
            total = total + row_slots[(d - 1) // 2, k].astype(F32)
        row[there] = total.astype(BF)
        if k:
            kv_swap.sending(k).start()
    kv_swap.keep()

    def near(u, c):
        values = products(u + 8)
        exchange(u).wait_recv()
        for which, value in enumerate(values):
            for k in range(2):
                cols = pl.ds(128 * which, 128)
                block = 2 * (u & 1) + k
                both = value[:, 128 * k : 128 * (k + 1)].astype(BF) + arrived[u >> 1, block, :, cols]
                arrived[u >> 1, block, :, cols] = both
        return c

    scatter_a = Scatter(arrived, 256, *ring_a)
    lax.fori_loop(0, 4, near, 0)
    scatter_a.start(0, 0)
    lax.fori_loop(4, 8, near, 0)
    scatter_a.start(1, 0)
    scatter_a.start(0, 1)
    scatter_a.start(1, 1)
    kv_swap.finish()
    for j in range(4):
        k_grad[:, pl.ds(128 * j, 128)] = kvg[j, pl.ds(0, 128)].T
        v_grad[:, pl.ds(128 * j, 128)] = kvg[j, pl.ds(128, 128)].T
    loads[3].wait()
    loads[4].wait()
    for n in range(4):
        rows = pl.ds(n * 256, 256)
        value = mm_cols(k_grad[...], v_key[rows, :]) + mm_cols(v_grad[...], v_value[rows, :])
        parts[:, rows] = value.astype(BF)
    total_d = HeadSum(parts, slots, d_enc, hs1, hr1, hs2, hr2)
    total_d.send()
    loads[0].wait()
    for d in (2, 1, 3):
        start = ((h + d) & 3) * 1024
        for n in range(4):
            out_send[d - 1, :, pl.ds(n * 256, 256)] = mm(mixed[...], v_attn[:, part(n, start)]).astype(BF)

    for n in range(4):
        here = part(n, h * 1024)
        out_own[:, pl.ds(n * 256, 256)] = mm(mixed[...], v_attn[:, here]) + v_dec[:, here].astype(F32)
    far_from, near_from = (1 - grp) * 512, grp * 512

    def put(left_t, right, row_at, base, target):
        for n in range(2):
            value = mm(left_t[part(n, base), :], right[...])
            for k in range(8):
                block = n * 8 + k
                for m in range(value.shape[1] // 512):
                    piece = value[32 * k : 32 * (k + 1), 512 * m : 512 * (m + 1)].astype(BF)
                    target[block // 4, block % 4, pl.ds(row_at + 32 * m, 32)] = piece

    def add(own, more):
        def body(b, c):
            own[b] = own[b] + more[b]
            return c

        lax.fori_loop(0, 4, body, 0)

    swap_b = partner_copy(stage_b, arrived_b, cs.at[0], cr.at[0])
    put(enc_t, k_grad, 0, far_from, stage_b)
    put(enc_t, v_grad, 32, far_from, stage_b)
    swap_b.start()
    put(enc_t, k_grad, 0, near_from, own_b)
    put(enc_t, v_grad, 32, near_from, own_b)
    total_d.share(total_d.receive())
    scatter_a.relay()
    swap_b.wait_recv()
    add(own_b, arrived_b)
    scatter_b = Scatter(own_b, 32, *ring_b)
    scatter_b.start_all()
    for load in loads[6:]:
        load.wait()
    normed_t[...] = v_normed[...].T
    total_d.collect()
    for d in (1, 3, 2):
        out_copy(d).start()
    d_enc_t[...] = d_enc[...].T
    swap_c = [partner_copy(stage_c[i], arrived_c[i], cs.at[1 + i], cr.at[1 + i]) for i in range(2)]
    put(d_enc_t, v_act, 0, far_from, stage_c[1])
    swap_c[1].start()
    for n in range(4):
        cols = pl.ds(n * 256, 256)
        pre = v_pre[:, cols]
        sig = 1.0 / (1.0 + jnp.exp(-pre))
        slope = sig * (1.0 + pre * (1.0 - sig))
        d_pre[:, cols] = (mm_cols(d_enc[...], v_out[cols, :]) * slope).astype(BF)
    scatter_b.relay()
    put(normed_t, d_pre, 0, far_from, stage_c[0])
    swap_c[0].start()
    scatters_c = [Scatter(own_c[i], 32, *rings) for i, rings in enumerate((ring_c, ring_d))]
    put(d_enc_t, v_act, 0, near_from, own_c[1])
    swap_c[1].wait_recv()
    add(own_c[1], arrived_c[1])
    scatters_c[1].start_all()
    put(normed_t, d_pre, 0, near_from, own_c[0])
    scatters_c[1].relay()
    swap_c[0].wait_recv()
    add(own_c[0], arrived_c[0])
    scatters_c[0].start_all()
    scatter_a.middle()
    scatters_c[0].relay()
    scatter_b.middle()
    for half in range(2):
        first[pl.ds(256 * half, 256)] = scatter_a.finish(half)
    for half in range(2):
        second[pl.ds(32 * half, 32)] = scatter_b.finish(half)
    scatters_c[1].middle()
    scatters_c[0].middle()
    total = out_own[...]
    for d in (1, 3, 2):
        out_copy(d).wait_recv()
        total = total + out_recv[d - 1].astype(F32)
    out[...] = total.astype(BF)
    m_swap.drain()
    kv_swap.drain()
    for k in range(4):
        for d in (1, 3):
            term(k, d).wait_send()
    for d in (1, 2, 3):
        out_copy(d).wait_send()

    def sent(u, c):
        exchange(u).wait_send()
        return c

    lax.fori_loop(0, 8, sent, 0)
    scatter_a.drain()
    scatter_b.drain()
    total_d.drain()
    for copy in (swap_b, *swap_c):
        copy.wait_send()
    for i in (1, 0):
        for half in range(2):
            second[pl.ds(64 + 64 * i + 32 * half, 32)] = scatters_c[i].finish(half)
    for scatter in scatters_c:
        scatter.drain()


def run_decoder(*args):
    sds = jax.ShapeDtypeStruct
    dma = pltpu.SemaphoreType.DMA
    return pl.pallas_call(
        decoder_kernel,
        out_shape=(sds((256, 1024), BF), sds((512, 256), F32), sds((192, 512), F32)),
        in_specs=[VM, VM] + [ANY] * 10,
        out_specs=(VM,) * 3,
        scratch_shapes=[
            *Scatter.scratch(256, 256), *Scatter.scratch(32, 512), *Scatter.scratch(32, 512), *Scatter.scratch(32, 512),
            pltpu.VMEM((256, 4096), BF), pltpu.VMEM((256, 4096), BF), pltpu.VMEM((512, 4096), BF),
            pltpu.VMEM((1024, 512), BF), pltpu.VMEM((1024, 512), BF), pltpu.VMEM((1024, 1024), BF),
            pltpu.VMEM((256, 1024), BF), pltpu.VMEM((256, 1024), BF), pltpu.VMEM((256, 1024), BF),
            pltpu.VMEM((256, 1024), F32), dma((10,)),
            pltpu.VMEM((4, 256, 256), BF), dma((3,)), dma((3,)),
            pltpu.VMEM((2, 4, 256, 256), BF), pltpu.VMEM((4, 256, 256), BF), dma((3, 4)), dma((3, 4)),
            pltpu.VMEM((4, 256, 256), BF), pltpu.VMEM((4, 256, 256), BF), dma((3,)), dma((3,)),
            pltpu.VMEM((256, 512), BF), pltpu.VMEM((512, 256), BF), pltpu.VMEM((512, 256), BF),
            pltpu.VMEM((256, 1024), F32), pltpu.VMEM((3, 256, 1024), BF), pltpu.VMEM((3, 256, 1024), BF),
            dma((3,)), dma((3,)),
            pltpu.VMEM((4, 4, 512, 256), BF), pltpu.VMEM((4, 4, 512, 256), BF), dma((8,)), dma((8,)),
            pltpu.VMEM((256, 512), BF), pltpu.VMEM((256, 512), BF),
            pltpu.VMEM((256, 1024), BF), pltpu.VMEM((3, 64, 1024), BF), pltpu.VMEM((256, 1024), BF),
            dma((3,)), dma((3,)), dma((3,)), dma((3,)),
            pltpu.VMEM((256, 1024), BF),
            *[pltpu.VMEM((4, 4, 64, 512), BF)] * 9,
            dma((3,)), dma((3,)),
            *[pltpu.VMEM((1024, 256), BF)] * 3,
        ],
        compiler_params=pltpu.CompilerParams(
            collective_id=1, has_side_effects=True, vmem_limit_bytes=VMEM_LIMIT
        ),
        cost_estimate=pl.CostEstimate(flops=7 * 10**9, bytes_accessed=24 * 2**20, transcendentals=2**18),
        name="decoder_scatter",
    )(*args)


def unpack_kernel(first, second, out_in, out, g_query, g_key, g_value, g_attn, g_in, g_out):
    out[...] = out_in[...]
    g_query[...] = first[:, pl.ds(0, 128)].T
    g_attn[...] = first[:, pl.ds(128, 128)]
    g_key[...] = second[pl.ds(0, 32)]
    g_value[...] = second[pl.ds(32, 32)]
    for n in range(2):
        cols = pl.ds(512 * n, 512)
        g_in[:, cols] = second[pl.ds(64 + 32 * n, 32)]
        g_out[:, cols] = second[pl.ds(128 + 32 * n, 32)]


def run_unpack(first, second, out):
    sds = jax.ShapeDtypeStruct
    return pl.pallas_call(
        unpack_kernel,
        out_shape=(
            sds((256, 1024), BF), sds((128, 512), F32), sds((32, 512), F32), sds((32, 512), F32),
            sds((512, 128), F32), sds((32, 1024), F32), sds((32, 1024), F32),
        ),
        in_specs=[VM] * 3,
        out_specs=(VM,) * 7,
        name="unpack",
    )(first, second, out)


def shards(
    enc_in, enc_gain, w_in, w_out, w_key, w_value, dec_in, w_query, w_attn_out, cotangent, group_doc, doc_lengths,
):
    normed, pre_act, activated, enc_out, kv, q_all, dm_all = run_encoder(
        enc_in[0], enc_gain[None, :], w_in, w_out, w_key, w_value, dec_in[0], w_query, w_attn_out, cotangent[0]
    )
    md, d_kv = run_attention(group_doc, doc_lengths, q_all, dm_all, kv)
    out, first, second = run_decoder(
        d_kv, md, dec_in[0], cotangent[0], w_attn_out, w_key, w_value, w_out, enc_out, normed, activated, pre_act
    )
    out, g_query, g_key, g_value, g_attn, g_in, g_out = run_unpack(first, second, out)
    return (out[None], g_query, g_key, g_value, g_attn, g_in, g_out.T)


def solution(mesh):
    placed = (
        P("grp", "seq", None),
        P(),
        P(None, "head"),
        P("head", None),
        P(None, "head"),
        P(None, "head"),
        P("grp", "seq", None),
        P(None, "head"),
        P("head", None),
        P("grp", "seq", None),
        P("grp", None),
        P("grp", None),
    )
    return jax.shard_map(
        shards,
        mesh=mesh,
        in_specs=placed,
        out_specs=(
            P("grp", "seq", "head"),
            P(("grp", "seq"), "head"),
            P(("grp", "seq"), "head"),
            P(("grp", "seq"), "head"),
            P("head", ("grp", "seq")),
            P(("grp", "seq"), "head"),
            P("head", ("grp", "seq")),
        ),
        check_vma=False,
    )
```
